128 devices in a mesh: member: 8 (over z, y_lo), space: 16 (over x, y_hi, core).
Axes of the slice: x: 4, y: 4 (y_hi: 2, y_lo: 2; y = y_hi * 2 + y_lo), z: 4, core: 2. Of those that a mesh axis runs over, the one named last changes fastest.
Arguments:
- ensemble: bfloat16 [256, 524288], P('member', 'space')
- analysis: float32 [524288], P('space'), may hold values from -6 to 6
Outputs:
- scaled_gradient: float32 [256, 524288], P('member', 'space')
The draws below stay inside these ranges and needn't reach their ends.
All inputs are finite; a program needn't handle non-finite values.
Results may differ from the reference program's by a relative error of at most 0.0003.
Values may be sent and summed in bfloat16 or wider, within the bound.
A program may use at most 128 MiB of HBM per device.

```python
import math
import jax
import jax.numpy as jnp
from jax import lax

MEMBERS = 256
POINTS = 524288


def draw_ensemble(key, part):
    key = jax.random.fold_in(key, 11)
    first = jax.random.fold_in(key, 0)
    second = jax.random.fold_in(key, 1)
    third = jax.random.fold_in(key, 2)
    fifth = jax.random.fold_in(key, 4)
    sixth = jax.random.fold_in(key, 5)
    seventh = jax.random.fold_in(key, 6)
    eighth = jax.random.fold_in(key, 7)
    member_scale = jnp.exp(jax.random.uniform(first, (MEMBERS, 1), jnp.float32, math.log(0.5), math.log(5.0)))
    position = jnp.arange(POINTS, dtype=jnp.float32) / POINTS
    point_scale = (1.0 + 2.0 * position) * jax.random.uniform(second, (POINTS,), jnp.float32, 0.6, 1.4)
    noise = jax.random.truncated_normal(third, -4.0, 4.0, (MEMBERS, POINTS), jnp.float32)
    order = jax.random.permutation(fifth, MEMBERS).astype(jnp.int32)
    partner = jnp.zeros((MEMBERS,), jnp.int32).at[order].set(jnp.roll(order, -1))
    mixing = jax.random.uniform(sixth, (MEMBERS, 1), jnp.float32, 0.4, 0.8)
    loadings = jax.random.uniform(seventh, (MEMBERS, 8), jnp.float32, -0.5, 0.5)
    latent = jax.random.normal(eighth, (8, POINTS), jnp.float32)
    core = noise + mixing * noise[partner]
    for index in range(8):
        core = core + loadings[:, index:index + 1] * latent[index][None, :]
    return (member_scale * point_scale[None, :] * (0.6 * core)).astype(jnp.bfloat16)


def steps_of(own_key, shape, shards, smallest, largest):
    def one(dim, blocks):
        draws = jax.random.uniform(jax.random.fold_in(jax.random.fold_in(own_key, 6), dim), (blocks,), jnp.float32, smallest / len(shards), largest / len(shards))
        return jnp.repeat(jnp.exp(draws), shape[dim] // blocks).reshape((-1,) + (1,) * (len(shape) - dim - 1))

    gain = one(*shards[0])
    for cut in shards[1:]:
        gain = gain * one(*cut)
    return gain


def scatter_about(stream_key, extent, scale, limit, pieces=(), kind=jnp.bfloat16):
    values = scale * jax.random.normal(stream_key, extent, jnp.float32)
    if pieces:
        values = values * steps_of(stream_key, extent, pieces, -0.22, 0.18)
    return jnp.clip(values, -limit, limit).astype(kind)


def setup_inputs(seed: int = 0) -> dict:
    seeds = jax.random.split(jax.random.key(seed), 3)
    ensemble = draw_ensemble(jax.random.fold_in(seeds[2], 71), 0)
    analysis = scatter_about(seeds[1], (POINTS,), 1.0, 6.0, ((0, 16),), jnp.float32)
    return dict(ensemble=ensemble, analysis=analysis)


def reference(ensemble, analysis):
    values = ensemble.astype(jnp.float32)
    deviation = values - analysis[None, :]
    obs_dist = jnp.sqrt(lax.optimization_barrier(jnp.sum(deviation * deviation, axis=1)))
    cross = jnp.dot(ensemble, ensemble.T, preferred_element_type=jnp.float32)
    square_norms = lax.optimization_barrier(jnp.sum(values * values, axis=1))
    pair_sq = square_norms[:, None] + square_norms[None, :] - 2.0 * cross
    rows_index = lax.broadcasted_iota(jnp.int32, (MEMBERS, MEMBERS), 0)
    cols_index = lax.broadcasted_iota(jnp.int32, (MEMBERS, MEMBERS), 1)
    on_diag = rows_index == cols_index
    safe_sq = jnp.where(on_diag, jnp.float32(1.0), pair_sq)
    weights = jnp.where(on_diag, jnp.float32(0.0), 1.0 / jnp.sqrt(safe_sq))
    row_total = lax.optimization_barrier(jnp.sum(weights, axis=1))
    weighted = jnp.dot(weights.astype(jnp.bfloat16), ensemble, preferred_element_type=jnp.float32)
    factor = jnp.float32(math.sqrt(POINTS))
    return factor * (deviation / obs_dist[:, None] - (row_total[:, None] * values - weighted) / MEMBERS)
```

```python
import functools
import math

import jax
import jax.numpy as jnp
from jax import lax
from jax.experimental import pallas as pl
from jax.experimental.pallas import tpu as pltpu
from jax.sharding import PartitionSpec as P

MESH = pl.DeviceIdType.MESH
F32 = jnp.float32
BF16 = jnp.bfloat16
RANGE = 250.0
SHIFT = 125.0
LN2 = math.log(2.0)
CHUNK = 512


def chunk_at(index):
    return pl.ds(pl.multiple_of(index * CHUNK, CHUNK), CHUNK)


def kernel(
    groups, chips, factor, x_hbm, a_hbm, out_hbm,
    gathered, own, analysis, weighted, sent, got, staged,
    part, part_in, chip_in, summed, low, totals, norms, obs_in,
    x_send, x_recv, p_send, p_recv, c_send, c_recv, s_send, s_recv, r_send, r_recv,
    o_send, o_recv, out_sem, local_sem,
):
    me = lax.axis_index("member")
    place = lax.axis_index("space")
    core = lax.rem(place, 2)
    chip = place // 2
    rank = me * 2 + core
    teams = groups * 2
    rows = own.shape[0]
    cols = gathered.shape[2]
    members = groups * rows
    steps = cols // CHUNK

    def columns(index):
        return pl.ds(pl.multiple_of(index * cols, cols), cols)

    def group_peer(d):
        other = lax.rem(me + d, groups)
        return other, (other, place)

    def team_peer(d):
        other = lax.rem(rank + d, teams)
        return other, (other // 2, chip * 2 + lax.rem(other, 2))

    def chip_peer(d):
        other = lax.rem(chip + d, chips)
        return other, (me, other * 2 + core)

    sibling = (me, chip * 2 + 1 - core)

    def remote(src, dst, send, recv, device):
        return pltpu.make_async_remote_copy(
            src_ref=src, dst_ref=dst, send_sem=send, recv_sem=recv,
            device_id=device, device_id_type=MESH,
        )

    load_analysis = pltpu.make_async_copy(a_hbm, analysis, local_sem.at[0])
    load_analysis.start()
    load_own = pltpu.make_async_copy(x_hbm, own, local_sem.at[1])
    load_own.start()
    keep = pltpu.make_async_copy(x_hbm.at[:, columns(me)], gathered.at[me], local_sem.at[2])
    keep.start()

    barrier = pltpu.get_barrier_semaphore()
    for d in range(1, teams):
        pl.semaphore_signal(barrier, inc=1, device_id=team_peer(d)[1], device_id_type=MESH)
    for d in range(1, chips):
        pl.semaphore_signal(barrier, inc=1, device_id=chip_peer(d)[1], device_id_type=MESH)
    pl.semaphore_wait(barrier, teams - 1 + chips - 1)

    spread = []
    for d in range(1, groups):
        other, device = group_peer(d)
        copy = remote(
            x_hbm.at[:, columns(other)], gathered.at[me], x_send.at[d], x_recv.at[d], device
        )
        copy.start()
        spread.append(copy)

    load_analysis.wait()
    load_own.wait()

    def add_distance(i, total):
        at = chunk_at(i)
        deviation = own[:, at].astype(F32) - analysis[:, at]
        square = deviation * deviation
        for k in range(CHUNK // 128):
            total = total + square[:, k * 128:(k + 1) * 128]
        return total

    distance = lax.fori_loop(0, own.shape[1] // CHUNK, add_distance, jnp.zeros((rows, 128), F32))
    obs_in[chips] = distance
    pair = remote(obs_in.at[chips], obs_in.at[chips + 1], o_send.at[0], o_recv.at[0], sibling)
    pair.start()
    pair.wait()
    obs_in[chip] = distance + obs_in[chips + 1]
    obs_copies = []
    for d in range(1, chips):
        other, device = chip_peer(d)
        copy = remote(obs_in.at[chip], obs_in.at[chip], o_send.at[d], o_recv.at[d], device)
        copy.start()
        obs_copies.append(copy)

    keep.wait()
    for copy in spread:
        copy.wait()

    def add_products(i, total):
        block = gathered[:, :, chunk_at(i)].reshape(members, CHUNK)
        return total + lax.dot_general(
            block, block, (((1,), (1,)), ((), ())), preferred_element_type=F32
        )

    cross = lax.fori_loop(0, steps, add_products, jnp.zeros((members, members), F32))
    row_index = lax.broadcasted_iota(jnp.int32, (members, members), 0)
    col_index = lax.broadcasted_iota(jnp.int32, (members, members), 1)
    diagonal = jnp.where(row_index == col_index, cross, 0.0)
    norm_rows = jnp.sum(diagonal, axis=1, keepdims=True)
    norm_cols = jnp.sum(diagonal, axis=0, keepdims=True)
    norms[...] = jnp.broadcast_to(norm_rows, (members, 128)).reshape(groups, rows, 128)
    pair_sq = norm_rows + norm_cols - 2.0 * cross
    half = members // 2
    small_row = lax.broadcasted_iota(jnp.int32, (half, half), 0)
    small_col = lax.broadcasted_iota(jnp.int32, (half, half), 1)
    upper = small_col > small_row
    lower = small_col < small_row
    share = members // teams
    part[: teams // 2] = pair_sq[:half, half:].reshape(teams // 2, share, half)
    part[teams // 2 :] = jnp.where(upper, pair_sq[:half, :half], pair_sq[half:, half:]).reshape(
        teams // 2, share, half
    )

    copies = []
    for d in range(1, teams):
        other, device = team_peer(d)
        copy = remote(part.at[other], part_in.at[rank], p_send.at[d], p_recv.at[d], device)
        copy.start()
        copies.append(copy)
    part_in[rank] = part[rank]
    for copy in copies:
        copy.wait()
    chip_in[chip] = jnp.sum(part_in[...], axis=0)
    copies = []
    for d in range(1, chips):
        other, device = chip_peer(d)
        copy = remote(chip_in.at[chip], chip_in.at[chip], c_send.at[d], c_recv.at[d], device)
        copy.start()
        copies.append(copy)
    for copy in copies:
        copy.wait()
    summed[rank] = jnp.sum(chip_in[...], axis=0)
    copies = []
    for d in range(1, teams):
        other, device = team_peer(d)
        copy = remote(summed.at[rank], summed.at[rank], s_send.at[d], s_recv.at[d], device)
        copy.start()
        copies.append(copy)
    for copy in copies:
        copy.wait()

    off = 1.0 / jnp.sqrt(summed[: teams // 2].reshape(half, half))
    triangles = summed[teams // 2 :].reshape(half, half)
    triangles = jnp.where(small_row == small_col, 1.0, triangles)
    triangles = 1.0 / jnp.sqrt(triangles)
    above = jnp.where(upper, triangles, 0.0)
    below = jnp.where(lower, triangles, 0.0)
    first = above + above.T
    second = below + below.T
    off_t = off.T
    low[:half, :half] = first.astype(BF16)
    low[:half, half:] = off.astype(BF16)
    low[half:, :half] = off_t.astype(BF16)
    low[half:, half:] = second.astype(BF16)
    total_first = jnp.sum(first + off, axis=1, keepdims=True)
    total_second = jnp.sum(second + off_t, axis=1, keepdims=True)
    groups_half = groups // 2
    totals[:groups_half] = jnp.broadcast_to(total_first, (half, 128)).reshape(groups_half, rows, 128)
    totals[groups_half:] = jnp.broadcast_to(total_second, (half, 128)).reshape(
        groups_half, rows, 128
    )

    def weigh(i, total):
        at = chunk_at(i)
        block = gathered[:, :, at].reshape(members, CHUNK)
        product = jnp.dot(low[...], block, preferred_element_type=F32)
        weighted[:, :, at] = product.reshape(groups, rows, CHUNK)
        along = product * block.astype(F32)
        for k in range(CHUNK // 128):
            total = total + along[:, k * 128:(k + 1) * 128]
        return total

    along = lax.fori_loop(0, steps, weigh, jnp.zeros((members, 128), F32))
    along = jnp.sum(along, axis=1, keepdims=True)
    square = norms[...].reshape(members, 128)[:, :1]
    slopes = jnp.where(square > 0.0, along / jnp.where(square > 0.0, square, 1.0), 0.0)
    slopes = slopes.astype(BF16).astype(F32)
    norms[...] = jnp.broadcast_to(slopes, (members, 128)).reshape(groups, rows, 128)

    returns = []
    for d in range(1, groups):
        other, device = group_peer(d)
        slope = norms[other][:, :1]

        def largest(i, top, other=other, slope=slope):
            at = chunk_at(i)
            rest = weighted[other, :, at] - slope * gathered[other, :, at].astype(F32)
            weighted[other, :, at] = rest
            rest = jnp.abs(rest)
            for k in range(CHUNK // 128):
                top = jnp.maximum(top, rest[:, k * 128:(k + 1) * 128])
            return top

        top = lax.fori_loop(0, steps, largest, jnp.zeros((rows, 128), F32))
        top = jnp.max(top, axis=1, keepdims=True)
        scale = jnp.maximum(top * 1.0079, 1e-30).astype(BF16).astype(F32)
        inverse = RANGE / scale

        def code(i, _, other=other, inverse=inverse):
            at = chunk_at(i)
            rest = weighted[other, :, at]
            size = jnp.exp2(jnp.abs(rest) * inverse - SHIFT)
            sent[other, :, at] = jnp.where(rest < 0.0, -size, size).astype(BF16)
            return 0

        lax.fori_loop(0, steps, code, 0)
        lane = lax.broadcasted_iota(jnp.int32, (rows, 128), 1)
        sent[other, :, cols:] = jnp.where(lane < 64, scale, slope).astype(BF16)
        copy = remote(sent.at[other], got.at[me], r_send.at[d], r_recv.at[d], device)
        copy.start()
        returns.append(copy)

    for copy in obs_copies:
        copy.wait()
    obs = jnp.sqrt(jnp.sum(jnp.sum(obs_in[:chips], axis=0), axis=1, keepdims=True))
    near = factor / obs
    row_total = totals[me][:, :1]

    def finish(piece, along_own, value_at):
        def one(i, _):
            at = chunk_at(i)
            point = pl.ds(pl.multiple_of(piece * cols + i * CHUNK, CHUNK), CHUNK)
            values = own[:, point].astype(F32)
            spread_term = value_at(at) - along_own * values
            staged[:, point] = (values - analysis[:, point]) * near + spread_term * (factor / members)
            return 0

        lax.fori_loop(0, steps, one, 0)
        copy = pltpu.make_async_copy(
            staged.at[:, columns(piece)], out_hbm.at[:, columns(piece)], out_sem.at[piece]
        )
        copy.start()

    finish(me, row_total, lambda at: weighted[me, :, at])
    for d in range(1, groups):
        returns[d - 1].wait()
        piece = lax.rem(me + groups - d, groups)
        scale = got[piece, :, cols:cols + 1].astype(F32) * (1.0 / (RANGE * LN2))
        slope = got[piece, :, cols + 64:cols + 65].astype(F32)

        def decode(at, piece=piece, scale=scale):
            coded = got[piece, :, at].astype(F32)
            size = (jnp.log(jnp.abs(coded)) + SHIFT * LN2) * scale
            return jnp.where(coded < 0.0, -size, size)

        finish(piece, row_total - slope, decode)
    for piece in range(groups):
        at = pl.ds(piece * cols, cols)
        pltpu.make_async_copy(staged.at[:, at], out_hbm.at[:, at], out_sem.at[piece]).wait()


def on_device(ensemble, analysis):
    rows, points = ensemble.shape
    groups = lax.axis_size("member")
    places = lax.axis_size("space")
    chips = places // 2
    teams = groups * 2
    members = rows * groups
    cols = points // groups
    half = members // 2
    share = members // teams
    factor = math.sqrt(points * places)
    dma = pltpu.SemaphoreType.DMA
    return pl.pallas_call(
        functools.partial(kernel, groups, chips, factor),
        out_shape=jax.ShapeDtypeStruct((rows, points), F32),
        in_specs=[pl.BlockSpec(memory_space=pltpu.HBM)] * 2,
        out_specs=pl.BlockSpec(memory_space=pltpu.HBM),
        scratch_shapes=[
            pltpu.VMEM((groups, rows, cols), BF16),
            pltpu.VMEM((rows, points), BF16),
            pltpu.VMEM((1, points), F32),
            pltpu.VMEM((groups, rows, cols), F32),
            pltpu.VMEM((groups, rows, cols + 128), BF16),
            pltpu.VMEM((groups, rows, cols + 128), BF16),
            pltpu.VMEM((rows, points), F32),
            pltpu.VMEM((teams, share, half), F32),
            pltpu.VMEM((teams, share, half), F32),
            pltpu.VMEM((chips, share, half), F32),
            pltpu.VMEM((teams, share, half), F32),
            pltpu.VMEM((members, members), BF16),
            pltpu.VMEM((groups, rows, 128), F32),
            pltpu.VMEM((groups, rows, 128), F32),
            pltpu.VMEM((chips + 2, rows, 128), F32),
            dma((groups,)), dma((groups,)),
            dma((teams,)), dma((teams,)),
            dma((chips,)), dma((chips,)),
            dma((teams,)), dma((teams,)),
            dma((groups,)), dma((groups,)),
            dma((chips,)), dma((chips,)),
            dma((groups,)), dma((3,)),
        ],
        compiler_params=pltpu.CompilerParams(
            collective_id=0, has_side_effects=True, vmem_limit_bytes=48 * 2**20
        ),
        cost_estimate=pl.CostEstimate(
            flops=4 * members * members * cols, bytes_accessed=8 * rows * points, transcendentals=0
        ),
    )(ensemble, analysis.reshape(1, points))


def solution(mesh):
    placed = (P("member", "space"), P("space"))
    return jax.shard_map(
        on_device, mesh=mesh, in_specs=placed, out_specs=P("member", "space"), check_vma=False
    )
```

```python
import functools
import math

import jax
import jax.numpy as jnp
from jax import lax
from jax.experimental import pallas as pl
from jax.experimental.pallas import tpu as pltpu
from jax.sharding import PartitionSpec as P

MESH = pl.DeviceIdType.MESH
F32 = jnp.float32
BF16 = jnp.bfloat16
RANGE = 250.0
SHIFT = 125.0
LN2 = math.log(2.0)
CHUNK = 512
PARTS = 2


def chunk_at(index):
    return pl.ds(pl.multiple_of(index * CHUNK, CHUNK), CHUNK)


def kernel(
    groups, chips, factor, x_hbm, a_hbm, out,
    gathered, own, analysis, weighted, sent, got,
    products, part, part_in, chip_in, summed, low, totals, lines, obs_in,
    x_send, x_recv, p_send, p_recv, c_send, c_recv, s_send, s_recv, r_send, r_recv,
    o_send, o_recv, local_sem,
):
    me = lax.axis_index("member")
    place = lax.axis_index("space")
    core = lax.rem(place, 2)
    chip = place // 2
    rank = me * 2 + core
    teams = groups * 2
    rows = own.shape[0]
    cols = gathered.shape[2]
    members = groups * rows
    width = cols // PARTS
    steps = width // CHUNK

    def columns(index):
        return pl.ds(pl.multiple_of(index * cols, cols), cols)

    def group_peer(d):
        other = lax.rem(me + d, groups)
        return other, (other, place)

    def team_peer(d):
        other = lax.rem(rank + d, teams)
        return other, (other // 2, chip * 2 + lax.rem(other, 2))

    def chip_peer(d):
        other = lax.rem(chip + d, chips)
        return other, (me, other * 2 + core)

    sibling = (me, chip * 2 + 1 - core)

    def remote(src, dst, send, recv, device):
        return pltpu.make_async_remote_copy(
            src_ref=src, dst_ref=dst, send_sem=send, recv_sem=recv,
            device_id=device, device_id_type=MESH,
        )

    load_analysis = pltpu.make_async_copy(a_hbm, analysis, local_sem.at[0])
    load_analysis.start()
    load_own = pltpu.make_async_copy(x_hbm, own, local_sem.at[1])
    load_own.start()
    keep = pltpu.make_async_copy(x_hbm.at[:, columns(me)], gathered.at[me], local_sem.at[2])
    keep.start()

    barrier = pltpu.get_barrier_semaphore()
    for d in range(1, teams):
        pl.semaphore_signal(barrier, inc=1, device_id=team_peer(d)[1], device_id_type=MESH)
    for d in range(1, chips):
        pl.semaphore_signal(barrier, inc=1, device_id=chip_peer(d)[1], device_id_type=MESH)
    pl.semaphore_wait(barrier, teams - 1 + chips - 1)

    spread = []
    for part_at in range(PARTS):
        for d in range(1, groups):
            other, device = group_peer(d)
            src = pl.ds(pl.multiple_of(other * cols + part_at * width, width), width)
            copy = remote(
                x_hbm.at[:, src], gathered.at[me, :, pl.ds(part_at * width, width)],
                x_send.at[part_at * groups + d], x_recv.at[part_at * groups + d], device,
            )
            copy.start()
            spread.append(copy)

    load_analysis.wait()
    load_own.wait()

    def add_distance(i, total):
        at = chunk_at(i)
        deviation = own[:, at].astype(F32) - analysis[:, at]
        square = deviation * deviation
        for k in range(CHUNK // 128):
            total = total + square[:, k * 128:(k + 1) * 128]
        return total

    distance = lax.fori_loop(0, own.shape[1] // CHUNK, add_distance, jnp.zeros((rows, 128), F32))
    obs_in[chips] = distance
    pair = remote(obs_in.at[chips], obs_in.at[chips + 1], o_send.at[0], o_recv.at[0], sibling)
    pair.start()
    pair.wait()
    obs_in[chip] = distance + obs_in[chips + 1]
    obs_copies = []
    for d in range(1, chips):
        other, device = chip_peer(d)
        copy = remote(obs_in.at[chip], obs_in.at[chip], o_send.at[d], o_recv.at[d], device)
        copy.start()
        obs_copies.append(copy)

    keep.wait()

    def add_products(i, _):
        block = gathered[:, :, chunk_at(i)].reshape(members, CHUNK)
        products[...] += lax.dot_general(
            block, block, (((1,), (1,)), ((), ())), preferred_element_type=F32
        )
        return 0

    products[...] = jnp.zeros_like(products)
    for part_at in range(PARTS):
        for copy in spread[part_at * (groups - 1):(part_at + 1) * (groups - 1)]:
            copy.wait_recv()
        lax.fori_loop(part_at * steps, (part_at + 1) * steps, add_products, 0)
    for copy in spread:
        copy.wait_send()
    cross = products[...]
    row_index = lax.broadcasted_iota(jnp.int32, (members, members), 0)
    col_index = lax.broadcasted_iota(jnp.int32, (members, members), 1)
    diagonal = jnp.where(row_index == col_index, cross, 0.0)
    norm_rows = jnp.sum(diagonal, axis=1, keepdims=True)
    norm_cols = jnp.sum(diagonal, axis=0, keepdims=True)
    pair_sq = norm_rows + norm_cols - 2.0 * cross
    half = members // 2
    small_row = lax.broadcasted_iota(jnp.int32, (half, half), 0)
    small_col = lax.broadcasted_iota(jnp.int32, (half, half), 1)
    upper = small_col > small_row
    lower = small_col < small_row
    share = members // teams
    part[: teams // 2] = pair_sq[:half, half:].reshape(teams // 2, share, half)
    part[teams // 2 :] = jnp.where(upper, pair_sq[:half, :half], pair_sq[half:, half:]).reshape(
        teams // 2, share, half
    )

    copies = []
    for d in range(1, teams):
        other, device = team_peer(d)
        copy = remote(part.at[other], part_in.at[rank], p_send.at[d], p_recv.at[d], device)
        copy.start()
        copies.append(copy)
    part_in[rank] = part[rank]
    for copy in copies:
        copy.wait()
    chip_in[chip] = jnp.sum(part_in[...], axis=0)
    copies = []
    for d in range(1, chips):
        other, device = chip_peer(d)
        copy = remote(chip_in.at[chip], chip_in.at[chip], c_send.at[d], c_recv.at[d], device)
        copy.start()
        copies.append(copy)
    for copy in copies:
        copy.wait()
    summed[rank] = jnp.sum(chip_in[...], axis=0)
    copies = []
    for d in range(1, teams):
        other, device = team_peer(d)
        copy = remote(summed.at[rank], summed.at[rank], s_send.at[d], s_recv.at[d], device)
        copy.start()
        copies.append(copy)
    for copy in copies:
        copy.wait()

    off = 1.0 / jnp.sqrt(summed[: teams // 2].reshape(half, half))
    triangles = summed[teams // 2 :].reshape(half, half)
    triangles = jnp.where(small_row == small_col, 1.0, triangles)
    triangles = 1.0 / jnp.sqrt(triangles)
    above = jnp.where(upper, triangles, 0.0)
    below = jnp.where(lower, triangles, 0.0)
    first = above + above.T
    second = below + below.T
    off_t = off.T
    low[:half, :half] = first.astype(BF16)
    low[:half, half:] = off.astype(BF16)
    low[half:, :half] = off_t.astype(BF16)
    low[half:, half:] = second.astype(BF16)
    total_first = jnp.sum(first + off, axis=1, keepdims=True)
    total_second = jnp.sum(second + off_t, axis=1, keepdims=True)
    groups_half = groups // 2
    totals[:groups_half] = jnp.broadcast_to(total_first, (half, 128)).reshape(groups_half, rows, 128)
    totals[groups_half:] = jnp.broadcast_to(total_second, (half, 128)).reshape(
        groups_half, rows, 128
    )

    def weigh(i, carry):
        along, square = carry
        at = chunk_at(i)
        block = gathered[:, :, at].reshape(members, CHUNK)
        product = jnp.dot(low[...], block, preferred_element_type=F32)
        weighted[:, :, at] = product.reshape(groups, rows, CHUNK)
        values = block.astype(F32)
        product = product * values
        values = values * values
        for k in range(CHUNK // 128):
            along = along + product[:, k * 128:(k + 1) * 128]
            square = square + values[:, k * 128:(k + 1) * 128]
        return along, square

    returns = []
    for part_at in range(PARTS):
        first_step, last_step = part_at * steps, (part_at + 1) * steps
        zeros = jnp.zeros((members, 128), F32)
        along, square = lax.fori_loop(first_step, last_step, weigh, (zeros, zeros))
        along = jnp.sum(along, axis=1, keepdims=True)
        square = jnp.sum(square, axis=1, keepdims=True)
        slopes = jnp.where(square > 0.0, along / jnp.where(square > 0.0, square, 1.0), 0.0)
        slopes = slopes.astype(BF16).astype(F32)
        lines[...] = jnp.broadcast_to(slopes, (members, 128)).reshape(groups, rows, 128)
        for d in range(1, groups):
            other, device = group_peer(d)
            slope = lines[other][:, :1]

            def largest(i, top, other=other, slope=slope):
                at = chunk_at(i)
                rest = weighted[other, :, at] - slope * gathered[other, :, at].astype(F32)
                weighted[other, :, at] = rest
                rest = jnp.abs(rest)
                for k in range(CHUNK // 128):
                    top = jnp.maximum(top, rest[:, k * 128:(k + 1) * 128])
                return top

            top = lax.fori_loop(first_step, last_step, largest, jnp.zeros((rows, 128), F32))
            top = jnp.max(top, axis=1, keepdims=True)
            scale = jnp.maximum(top * 1.0079, 1e-30).astype(BF16).astype(F32)
            inverse = RANGE / scale

            def code(i, _, other=other, inverse=inverse, part_at=part_at):
                rest = weighted[other, :, chunk_at(i + part_at * steps)]
                size = jnp.exp2(jnp.abs(rest) * inverse - SHIFT)
                sent[part_at, other, :, chunk_at(i)] = jnp.where(rest < 0.0, -size, size).astype(BF16)
                return 0

            lax.fori_loop(0, steps, code, 0)
            lane = lax.broadcasted_iota(jnp.int32, (rows, 128), 1)
            sent[part_at, other, :, width:] = jnp.where(lane < 64, scale, slope).astype(BF16)
            at = part_at * groups + d
            copy = remote(
                sent.at[part_at, other], got.at[part_at, me], r_send.at[at], r_recv.at[at], device
            )
            copy.start()
            returns.append(copy)

    for copy in obs_copies:
        copy.wait()
    obs = jnp.sqrt(jnp.sum(jnp.sum(obs_in[:chips], axis=0), axis=1, keepdims=True))
    near = factor / obs
    row_total = totals[me][:, :1]

    def finish(piece, offset, count, along_own, value_at):
        def one(i, _):
            point = pl.ds(pl.multiple_of(piece * cols + offset + i * CHUNK, CHUNK), CHUNK)
            values = own[:, point].astype(F32)
            spread_term = value_at(chunk_at(i)) - along_own * values
            out[:, point] = (values - analysis[:, point]) * near + spread_term * (factor / members)
            return 0

        lax.fori_loop(0, count, one, 0)

    finish(me, 0, cols // CHUNK, row_total, lambda at: weighted[me, :, at])
    for part_at in range(PARTS):
        for d in range(1, groups):
            returns[part_at * (groups - 1) + d - 1].wait()
            piece = lax.rem(me + groups - d, groups)
            scale = got[part_at, piece, :, width:width + 1].astype(F32) * (1.0 / (RANGE * LN2))
            slope = got[part_at, piece, :, width + 64:width + 65].astype(F32)

            def decode(at, piece=piece, scale=scale, part_at=part_at):
                coded = got[part_at, piece, :, at].astype(F32)
                size = (jnp.log(jnp.abs(coded)) + SHIFT * LN2) * scale
                return jnp.where(coded < 0.0, -size, size)

            finish(piece, part_at * width, steps, row_total - slope, decode)


def on_device(ensemble, analysis):
    rows, points = ensemble.shape
    groups = lax.axis_size("member")
    places = lax.axis_size("space")
    chips = places // 2
    teams = groups * 2
    members = rows * groups
    cols = points // groups
    half = members // 2
    share = members // teams
    factor = math.sqrt(points * places)
    dma = pltpu.SemaphoreType.DMA
    return pl.pallas_call(
        functools.partial(kernel, groups, chips, factor),
        out_shape=pltpu.VMEM((rows, points), F32),
        in_specs=[pl.BlockSpec(memory_space=pltpu.HBM)] * 2,
        out_specs=pl.BlockSpec(memory_space=pltpu.VMEM),
        scratch_shapes=[
            pltpu.VMEM((groups, rows, cols), BF16),
            pltpu.VMEM((rows, points), BF16),
            pltpu.VMEM((1, points), F32),
            pltpu.VMEM((groups, rows, cols), F32),
            pltpu.VMEM((PARTS, groups, rows, cols // PARTS + 128), BF16),
            pltpu.VMEM((PARTS, groups, rows, cols // PARTS + 128), BF16),
            pltpu.VMEM((members, members), F32),
            pltpu.VMEM((teams, share, half), F32),
            pltpu.VMEM((teams, share, half), F32),
            pltpu.VMEM((chips, share, half), F32),
            pltpu.VMEM((teams, share, half), F32),
            pltpu.VMEM((members, members), BF16),
            pltpu.VMEM((groups, rows, 128), F32),
            pltpu.VMEM((groups, rows, 128), F32),
            pltpu.VMEM((chips + 2, rows, 128), F32),
            dma((PARTS * groups,)), dma((PARTS * groups,)),
            dma((teams,)), dma((teams,)),
            dma((chips,)), dma((chips,)),
            dma((teams,)), dma((teams,)),
            dma((PARTS * groups,)), dma((PARTS * groups,)),
            dma((chips,)), dma((chips,)),
            dma((3,)),
        ],
        compiler_params=pltpu.CompilerParams(
            collective_id=0, has_side_effects=True, vmem_limit_bytes=56 * 2**20
        ),
        cost_estimate=pl.CostEstimate(
            flops=4 * members * members * cols, bytes_accessed=8 * rows * points, transcendentals=0
        ),
    )(ensemble, analysis.reshape(1, points))


def solution(mesh):
    placed = (P("member", "space"), P("space"))
    return jax.shard_map(
        on_device, mesh=mesh, in_specs=placed, out_specs=P("member", "space"), check_vma=False
    )
```

```python
import functools
import math

import jax
import jax.numpy as jnp
from jax import lax
from jax.experimental import pallas as pl
from jax.experimental.pallas import tpu as pltpu
from jax.sharding import PartitionSpec as P

MESH = pl.DeviceIdType.MESH
F32 = jnp.float32
BF16 = jnp.bfloat16
RANGE = 250.0
SHIFT = 125.0
LN2 = math.log(2.0)
CHUNK = 512
SPREAD = (4, 3, 1)
RETURN = ((2,), (3, 2, 1))
TILE = 128


def chunk_at(index):
    return pl.ds(pl.multiple_of(index * CHUNK, CHUNK), CHUNK)


def kernel(
    groups, chips, factor, x_hbm, a_hbm, out,
    gathered, own, analysis, weighted, sent, got,
    products, part, part_in, chip_in, summed, low, totals, lines, obs_in,
    x_send, x_recv, p_send, p_recv, c_send, c_recv, s_send, s_recv, r_send, r_recv,
    o_send, o_recv, local_sem,
):
    me = lax.axis_index("member")
    place = lax.axis_index("space")
    core = lax.rem(place, 2)
    chip = place // 2
    rank = me * 2 + core
    teams = groups * 2
    rows = own.shape[0]
    cols = gathered.shape[2]
    members = groups * rows
    unit = cols // 8
    steps = unit // CHUNK

    def columns(index):
        return pl.ds(pl.multiple_of(index * cols, cols), cols)

    def group_peer(d):
        other = lax.rem(me + d, groups)
        return other, (other, place)

    def team_peer(d):
        other = lax.rem(rank + d, teams)
        return other, (other // 2, chip * 2 + lax.rem(other, 2))

    def chip_peer(d):
        other = lax.rem(chip + d, chips)
        return other, (me, other * 2 + core)

    sibling = (me, chip * 2 + 1 - core)

    def remote(src, dst, send, recv, device):
        return pltpu.make_async_remote_copy(
            src_ref=src, dst_ref=dst, send_sem=send, recv_sem=recv,
            device_id=device, device_id_type=MESH,
        )

    barrier = pltpu.get_barrier_semaphore()
    for d in range(1, teams):
        pl.semaphore_signal(barrier, inc=1, device_id=team_peer(d)[1], device_id_type=MESH)
    for d in range(1, chips):
        pl.semaphore_signal(barrier, inc=1, device_id=chip_peer(d)[1], device_id_type=MESH)

    load_analysis = pltpu.make_async_copy(a_hbm, analysis, local_sem.at[0])
    load_analysis.start()
    load_own = pltpu.make_async_copy(x_hbm, own, local_sem.at[1])
    load_own.start()
    keep = pltpu.make_async_copy(x_hbm.at[:, columns(me)], gathered.at[me], local_sem.at[2])
    keep.start()

    pl.semaphore_wait(barrier, teams - 1 + chips - 1)

    spread = []
    start = 0
    for index, eighths in enumerate(SPREAD):
        width = eighths * unit
        for d in range(1, groups):
            other, device = group_peer(d)
            src = pl.ds(pl.multiple_of(other * cols + start * unit, unit), width)
            copy = remote(
                x_hbm.at[:, src], gathered.at[me, :, pl.ds(start * unit, width)],
                x_send.at[index * groups + d], x_recv.at[index * groups + d], device,
            )
            copy.start()
            spread.append(copy)
        start += eighths

    load_analysis.wait()
    load_own.wait()

    def add_distance(i, total):
        at = chunk_at(i)
        deviation = own[:, at].astype(F32) - analysis[:, at]
        square = deviation * deviation
        for k in range(CHUNK // 128):
            total = total + square[:, k * 128:(k + 1) * 128]
        return total

    distance = lax.fori_loop(0, own.shape[1] // CHUNK, add_distance, jnp.zeros((rows, 128), F32))
    obs_in[chips] = distance
    pair = remote(obs_in.at[chips], obs_in.at[chips + 1], o_send.at[0], o_recv.at[0], sibling)
    pair.start()
    pair.wait()
    obs_in[chip] = distance + obs_in[chips + 1]
    obs_copies = []
    for d in range(1, chips):
        other, device = chip_peer(d)
        copy = remote(obs_in.at[chip], obs_in.at[chip], o_send.at[d], o_recv.at[d], device)
        copy.start()
        obs_copies.append(copy)

    keep.wait()

    def add_products(i, _):
        block = gathered[:, :, chunk_at(i)].reshape(members, CHUNK)
        products[...] += lax.dot_general(
            block, block, (((1,), (1,)), ((), ())), preferred_element_type=F32
        )
        return 0

    products[...] = jnp.zeros_like(products)
    start = 0
    for index, eighths in enumerate(SPREAD):
        for copy in spread[index * (groups - 1):(index + 1) * (groups - 1)]:
            copy.wait_recv()
        lax.fori_loop(start * steps, (start + eighths) * steps, add_products, 0)
        start += eighths
    cross = products[...]
    row_index = lax.broadcasted_iota(jnp.int32, (members, members), 0)
    col_index = lax.broadcasted_iota(jnp.int32, (members, members), 1)
    diagonal = jnp.where(row_index == col_index, cross, 0.0)
    norm_rows = jnp.sum(diagonal, axis=1, keepdims=True)
    norm_cols = jnp.sum(diagonal, axis=0, keepdims=True)
    pair_sq = norm_rows + norm_cols - 2.0 * cross
    half = members // 2
    small_row = lax.broadcasted_iota(jnp.int32, (half, half), 0)
    small_col = lax.broadcasted_iota(jnp.int32, (half, half), 1)
    upper = small_col > small_row
    lower = small_col < small_row
    share = members // teams
    part[: teams // 2] = pair_sq[:half, half:].reshape(teams // 2, share, half)
    part[teams // 2 :] = jnp.where(upper, pair_sq[:half, :half], pair_sq[half:, half:]).reshape(
        teams // 2, share, half
    )

    pending = list(spread)
    copies = []
    for d in range(1, teams):
        other, device = team_peer(d)
        copy = remote(part.at[other], part_in.at[rank], p_send.at[d], p_recv.at[d], device)
        copy.start()
        copies.append(copy)
    part_in[rank] = part[rank]
    for copy in copies:
        copy.wait_recv()
    pending += copies
    chip_in[chip] = jnp.sum(part_in[...], axis=0)
    copies = []
    for d in range(1, chips):
        other, device = chip_peer(d)
        copy = remote(chip_in.at[chip], chip_in.at[chip], c_send.at[d], c_recv.at[d], device)
        copy.start()
        copies.append(copy)
    for copy in copies:
        copy.wait_recv()
    pending += copies
    summed[rank] = jnp.sum(chip_in[...], axis=0)
    copies = []
    for d in range(1, teams):
        other, device = team_peer(d)
        copy = remote(summed.at[rank], summed.at[rank], s_send.at[d], s_recv.at[d], device)
        copy.start()
        copies.append(copy)
    for copy in copies:
        copy.wait_recv()
    pending += copies

    off = 1.0 / jnp.sqrt(summed[: teams // 2].reshape(half, half))
    triangles = summed[teams // 2 :].reshape(half, half)
    triangles = jnp.where(small_row == small_col, 1.0, triangles)
    triangles = 1.0 / jnp.sqrt(triangles)
    above = jnp.where(upper, triangles, 0.0)
    below = jnp.where(lower, triangles, 0.0)
    first = above + above.T
    second = below + below.T
    off_t = off.T
    low[:half, :half] = first.astype(BF16)
    low[:half, half:] = off.astype(BF16)
    low[half:, :half] = off_t.astype(BF16)
    low[half:, half:] = second.astype(BF16)
    total_first = jnp.sum(first + off, axis=1, keepdims=True)
    total_second = jnp.sum(second + off_t, axis=1, keepdims=True)
    groups_half = groups // 2
    totals[:groups_half] = jnp.broadcast_to(total_first, (half, 128)).reshape(groups_half, rows, 128)
    totals[groups_half:] = jnp.broadcast_to(total_second, (half, 128)).reshape(
        groups_half, rows, 128
    )

    def weigh(i, carry):
        along, square = carry
        at = chunk_at(i)
        block = gathered[:, :, at].reshape(members, CHUNK)
        product = jnp.dot(low[...], block, preferred_element_type=F32)
        weighted[:, :, at] = product.reshape(groups, rows, CHUNK)
        values = block.astype(F32)
        product = product * values
        values = values * values
        for k in range(CHUNK // 128):
            along = along + product[:, k * 128:(k + 1) * 128]
            square = square + values[:, k * 128:(k + 1) * 128]
        return along, square

    share_rows = rows // 2
    lane = lax.broadcasted_iota(jnp.int32, (share_rows, TILE), 1)
    returns = []

    def give(message, base, size, d):
        other, device = group_peer(d)
        at = message * groups + d
        span = pl.ds(base, size)
        copy = remote(
            sent.at[other, :, span], got.at[me, :, span], r_send.at[at], r_recv.at[at], device
        )
        copy.start()
        returns.append(copy)

    start, base, message = 0, 0, 0
    for parts in RETURN:
        first_step, last_step = start * steps, (start + sum(parts)) * steps
        zeros = jnp.zeros((members, 128), F32)
        along, square = lax.fori_loop(first_step, last_step, weigh, (zeros, zeros))
        along = jnp.sum(along, axis=1, keepdims=True)
        square = jnp.sum(square, axis=1, keepdims=True)
        slopes = jnp.where(square > 0.0, along / jnp.where(square > 0.0, square, 1.0), 0.0)
        slopes = slopes.astype(BF16).astype(F32)
        lines[...] = jnp.broadcast_to(slopes, (members, 128)).reshape(groups, rows, 128)
        for d in range(1, groups):
            other, device = group_peer(d)
            slope = lines[other][:, :1]

            def largest(i, top, other=other, slope=slope):
                at = chunk_at(i)
                rest = weighted[other, :, at] - slope * gathered[other, :, at].astype(F32)
                weighted[other, :, at] = rest
                rest = jnp.abs(rest)
                for k in range(CHUNK // 128):
                    top = jnp.maximum(top, rest[:, k * 128:(k + 1) * 128])
                return top

            top = lax.fori_loop(first_step, last_step, largest, jnp.zeros((rows, 128), F32))
            top = jnp.max(top, axis=1, keepdims=True)
            scale = jnp.maximum(top * 1.0079, 1e-30).astype(BF16).astype(F32)
            inverse = RANGE / scale
            heads = jnp.where(lane < 32, scale[:share_rows], slope[:share_rows])
            tails = jnp.where(lane < 96, scale[share_rows:], slope[share_rows:])
            sent[other, :, base:base + TILE] = jnp.where(lane < 64, heads, tails).astype(BF16)
            place_at, step_at = base + TILE, first_step
            for eighths in parts:
                width = eighths * unit

                def code(i, _, other=other, inverse=inverse, place_at=place_at, step_at=step_at, width=width):
                    rest = weighted[other, :, chunk_at(i + step_at)]
                    size = jnp.exp2(jnp.abs(rest) * inverse - SHIFT)
                    coded = jnp.where(rest < 0.0, -size, size).astype(BF16)
                    early = pl.ds(pl.multiple_of(place_at + i * CHUNK, 128), CHUNK)
                    late = pl.ds(pl.multiple_of(place_at + width + i * CHUNK, 128), CHUNK)
                    sent[other, :, early] = coded[:share_rows]
                    sent[other, :, late] = coded[share_rows:]
                    return 0

                lax.fori_loop(0, eighths * steps, code, 0)
                place_at, step_at = place_at + 2 * width, step_at + eighths * steps
            give(message, base, TILE + 2 * parts[0] * unit, d)
        base += TILE + 2 * parts[0] * unit
        message += 1
        for eighths in parts[1:]:
            for d in range(1, groups):
                give(message, base, 2 * eighths * unit, d)
            base += 2 * eighths * unit
            message += 1
        start += sum(parts)

    for copy in obs_copies:
        copy.wait()
    obs = jnp.sqrt(jnp.sum(jnp.sum(obs_in[:chips], axis=0), axis=1, keepdims=True))
    near = factor / obs
    share_factor = factor / members
    row_total = totals[me][:, :1]

    def finish(piece, offset, count, along_own, value_at):
        def one(i, _):
            point = pl.ds(pl.multiple_of(piece * cols + offset + i * CHUNK, CHUNK), CHUNK)
            out[:, point] = own[:, point].astype(F32) * along_own - analysis[:, point] * near + value_at(i)
            return 0

        lax.fori_loop(0, count, one, 0)

    finish(
        me, 0, cols // CHUNK, near - row_total * share_factor,
        lambda i: weighted[me, :, chunk_at(i)] * share_factor,
    )
    start, base, message = 0, 0, 0
    for parts in RETURN:
        tile_at = base
        base += TILE
        for eighths in parts:
            width = eighths * unit
            for d in range(1, groups):
                copy = returns[message * (groups - 1) + d - 1]
                copy.wait_recv()
                pending.append(copy)
                piece = lax.rem(me + groups - d, groups)
                tile = got[piece, :, tile_at:tile_at + TILE].astype(F32)
                scale = jnp.concatenate([tile[:, :1], tile[:, 64:65]], axis=0)
                scale = scale * (share_factor / (RANGE * LN2))
                slope = jnp.concatenate([tile[:, 32:33], tile[:, 96:97]], axis=0)

                def decode(i, piece=piece, scale=scale, base=base, width=width):
                    early = pl.ds(pl.multiple_of(base + i * CHUNK, 128), CHUNK)
                    late = pl.ds(pl.multiple_of(base + width + i * CHUNK, 128), CHUNK)
                    coded = jnp.concatenate([got[piece, :, early], got[piece, :, late]], axis=0)
                    coded = coded.astype(F32)
                    size = (jnp.log(jnp.abs(coded)) + SHIFT * LN2) * scale
                    return jnp.where(coded < 0.0, -size, size)

                finish(
                    piece, start * unit, eighths * steps,
                    near - (row_total - slope) * share_factor, decode,
                )
            base += 2 * width
            start += eighths
            message += 1
    for copy in pending:
        copy.wait_send()


def on_device(ensemble, analysis):
    rows, points = ensemble.shape
    groups = lax.axis_size("member")
    places = lax.axis_size("space")
    chips = places // 2
    teams = groups * 2
    members = rows * groups
    cols = points // groups
    half = members // 2
    share = members // teams
    factor = math.sqrt(points * places)
    messages = sum(len(parts) for parts in RETURN)
    dma = pltpu.SemaphoreType.DMA
    return pl.pallas_call(
        functools.partial(kernel, groups, chips, factor),
        out_shape=pltpu.VMEM((rows, points), F32),
        in_specs=[pl.BlockSpec(memory_space=pltpu.HBM)] * 2,
        out_specs=pl.BlockSpec(memory_space=pltpu.VMEM),
        scratch_shapes=[
            pltpu.VMEM((groups, rows, cols), BF16),
            pltpu.VMEM((rows, points), BF16),
            pltpu.VMEM((1, points), F32),
            pltpu.VMEM((groups, rows, cols), F32),
            pltpu.VMEM((groups, rows // 2, 2 * cols + len(RETURN) * TILE), BF16),
            pltpu.VMEM((groups, rows // 2, 2 * cols + len(RETURN) * TILE), BF16),
            pltpu.VMEM((members, members), F32),
            pltpu.VMEM((teams, share, half), F32),
            pltpu.VMEM((teams, share, half), F32),
            pltpu.VMEM((chips, share, half), F32),
            pltpu.VMEM((teams, share, half), F32),
            pltpu.VMEM((members, members), BF16),
            pltpu.VMEM((groups, rows, 128), F32),
            pltpu.VMEM((groups, rows, 128), F32),
            pltpu.VMEM((chips + 2, rows, 128), F32),
            dma((len(SPREAD) * groups,)), dma((len(SPREAD) * groups,)),
            dma((teams,)), dma((teams,)),
            dma((chips,)), dma((chips,)),
            dma((teams,)), dma((teams,)),
            dma((messages * groups,)), dma((messages * groups,)),
            dma((chips,)), dma((chips,)),
            dma((3,)),
        ],
        compiler_params=pltpu.CompilerParams(
            collective_id=0, has_side_effects=True, vmem_limit_bytes=56 * 2**20
        ),
        cost_estimate=pl.CostEstimate(
            flops=4 * members * members * cols, bytes_accessed=8 * rows * points, transcendentals=0
        ),
    )(ensemble, analysis.reshape(1, points))


def solution(mesh):
    placed = (P("member", "space"), P("space"))
    return jax.shard_map(
        on_device, mesh=mesh, in_specs=placed, out_specs=P("member", "space"), check_vma=False
    )
```

```python
import functools
import math

import jax
import jax.numpy as jnp
from jax import lax
from jax.experimental import pallas as pl
from jax.experimental.pallas import tpu as pltpu
from jax.sharding import PartitionSpec as P

MESH = pl.DeviceIdType.MESH
F32 = jnp.float32
BF16 = jnp.bfloat16
RANGE = 250.0
SHIFT = 125.0
LN2 = math.log(2.0)
CHUNK = 512
SPREAD = (2, 2, 2, 2)
RETURN = ((1,), (2, 2, 2, 1))
TILE = 128


def chunk_at(index):
    return pl.ds(pl.multiple_of(index * CHUNK, CHUNK), CHUNK)


def wide(tile):
    return jnp.concatenate([tile] * (CHUNK // 128), axis=1)


def kernel(
    groups, chips, factor, x_hbm, a_hbm, out,
    gathered, own, analysis, weighted, sent, got,
    products, part, part_in, chip_in, summed, low, totals, lines, inverses, obs_in,
    x_send, x_recv, p_send, p_recv, c_send, c_recv, s_send, s_recv, r_send, r_recv,
    o_send, o_recv, local_sem,
):
    me = lax.axis_index("member")
    place = lax.axis_index("space")
    core = lax.rem(place, 2)
    chip = place // 2
    rank = me * 2 + core
    teams = groups * 2
    rows = own.shape[0]
    cols = gathered.shape[2]
    members = groups * rows
    unit = cols // 8
    steps = unit // CHUNK

    def each(count, body):
        for d in range(1, count):
            body(d)

    def loop(count, body):
        lax.fori_loop(1, count, lambda d, _: (body(d), 0)[1], 0)

    def columns(index):
        return pl.ds(pl.multiple_of(index * cols, cols), cols)

    def group_peer(d):
        other = lax.rem(me // 2 + 2 * groups - d, groups // 2) * 2 + lax.rem(me + (groups - d) // (groups // 2), 2)
        return other, (other, place)

    def group_source(d):
        return lax.rem(me // 2 + d, groups // 2) * 2 + lax.rem(me + (groups - d) // (groups // 2), 2)

    def team_peer(d):
        other = lax.rem(rank + d, teams)
        return other, (other // 2, chip * 2 + lax.rem(other, 2))

    def chip_peer(d):
        other = lax.rem(chip + d, chips)
        return other, (me, other * 2 + core)

    sibling = (me, chip * 2 + 1 - core)

    def remote(src, dst, send, recv, device):
        return pltpu.make_async_remote_copy(
            src_ref=src, dst_ref=dst, send_sem=send, recv_sem=recv,
            device_id=device, device_id_type=MESH,
        )

    barrier = pltpu.get_barrier_semaphore()

    def greet(device):
        pl.semaphore_signal(barrier, inc=1, device_id=device, device_id_type=MESH)

    each(teams, lambda d: greet(team_peer(d)[1]))
    each(chips, lambda d: greet(chip_peer(d)[1]))

    load_analysis = pltpu.make_async_copy(a_hbm, analysis, local_sem.at[0])
    load_analysis.start()
    load_own = pltpu.make_async_copy(x_hbm, own, local_sem.at[1])
    load_own.start()
    keep = pltpu.make_async_copy(x_hbm.at[:, columns(me)], gathered.at[me], local_sem.at[2])
    keep.start()

    pl.semaphore_wait(barrier, teams - 1 + chips - 1)

    def spread(index, start, d):
        width = SPREAD[index] * unit
        other, device = group_peer(d)
        src = pl.ds(pl.multiple_of(other * cols + start * unit, unit), width)
        at = index * groups + d
        return remote(
            x_hbm.at[:, src], gathered.at[me, :, pl.ds(start * unit, width)],
            x_send.at[at], x_recv.at[at], device,
        )

    start = 0
    for index, eighths in enumerate(SPREAD):
        each(groups, lambda d: spread(index, start, d).start())
        start += eighths

    load_analysis.wait()
    load_own.wait()

    def add_distance(i, total):
        at = chunk_at(i)
        deviation = own[:, at].astype(F32) - analysis[:, at]
        square = deviation * deviation
        for k in range(CHUNK // 128):
            total = total + square[:, k * 128:(k + 1) * 128]
        return total

    distance = lax.fori_loop(0, own.shape[1] // CHUNK, add_distance, jnp.zeros((rows, 128), F32))
    obs_in[chips] = distance
    pair = remote(obs_in.at[chips], obs_in.at[chips + 1], o_send.at[0], o_recv.at[0], sibling)
    pair.start()
    pair.wait()
    obs_in[chip] = distance + obs_in[chips + 1]

    def obs_copy(d):
        return remote(
            obs_in.at[chip], obs_in.at[chip], o_send.at[d], o_recv.at[d], chip_peer(d)[1]
        )

    each(chips, lambda d: obs_copy(d).start())
    keep.wait()

    def add_products(i, _):
        block = gathered[:, :, chunk_at(i)].reshape(members, CHUNK)
        products[...] += lax.dot_general(
            block, block, (((1,), (1,)), ((), ())), preferred_element_type=F32
        )
        return 0

    products[...] = jnp.zeros_like(products)
    start = 0
    for index, eighths in enumerate(SPREAD):
        each(groups, lambda d: spread(index, start, d).wait_recv())
        lax.fori_loop(start * steps, (start + eighths) * steps, add_products, 0)
        start += eighths
    cross = products[...]
    row_index = lax.broadcasted_iota(jnp.int32, (members, members), 0)
    col_index = lax.broadcasted_iota(jnp.int32, (members, members), 1)
    diagonal = jnp.where(row_index == col_index, cross, 0.0)
    norm_rows = jnp.sum(diagonal, axis=1, keepdims=True)
    norm_cols = jnp.sum(diagonal, axis=0, keepdims=True)
    pair_sq = norm_rows + norm_cols - 2.0 * cross
    half = members // 2
    small_row = lax.broadcasted_iota(jnp.int32, (half, half), 0)
    small_col = lax.broadcasted_iota(jnp.int32, (half, half), 1)
    upper = small_col > small_row
    lower = small_col < small_row
    share = members // teams
    part[: teams // 2] = pair_sq[:half, half:].reshape(teams // 2, share, half)
    part[teams // 2 :] = jnp.where(upper, pair_sq[:half, :half], pair_sq[half:, half:]).reshape(
        teams // 2, share, half
    )

    def part_copy(d):
        other, device = team_peer(d)
        return remote(part.at[other], part_in.at[rank], p_send.at[d], p_recv.at[d], device)

    def chip_copy(d):
        return remote(
            chip_in.at[chip], chip_in.at[chip], c_send.at[d], c_recv.at[d], chip_peer(d)[1]
        )

    def sum_copy(d):
        return remote(
            summed.at[rank], summed.at[rank], s_send.at[d], s_recv.at[d], team_peer(d)[1]
        )

    each(teams, lambda d: part_copy(d).start())
    part_in[rank] = part[rank]
    each(teams, lambda d: part_copy(d).wait_recv())
    chip_in[chip] = jnp.sum(part_in[...], axis=0)
    each(chips, lambda d: chip_copy(d).start())
    each(chips, lambda d: chip_copy(d).wait_recv())
    summed[rank] = jnp.sum(chip_in[...], axis=0)
    each(teams, lambda d: sum_copy(d).start())
    each(teams, lambda d: sum_copy(d).wait_recv())

    off = 1.0 / jnp.sqrt(summed[: teams // 2].reshape(half, half))
    triangles = summed[teams // 2 :].reshape(half, half)
    triangles = jnp.where(small_row == small_col, 1.0, triangles)
    triangles = 1.0 / jnp.sqrt(triangles)
    above = jnp.where(upper, triangles, 0.0)
    below = jnp.where(lower, triangles, 0.0)
    first = above + above.T
    second = below + below.T
    off_t = off.T
    def slope_of(own_part, own_products, cross_part, cross_products):
        along = jnp.sum(own_part * own_products + cross_part * cross_products, axis=1, keepdims=True)
        square = jnp.sum(jnp.where(small_row == small_col, own_products, 0.0), axis=1, keepdims=True)
        slope = jnp.where(square > 0.0, along / jnp.where(square > 0.0, square, 1.0), 0.0)
        return slope.astype(BF16).astype(F32)

    slope_first = slope_of(first, products[:half, :half], off, products[:half, half:])
    slope_second = slope_of(second, products[half:, half:], off_t, products[half:, :half])
    low[:half, :half] = jnp.where(small_row == small_col, -slope_first, first).astype(BF16)
    low[:half, half:] = off.astype(BF16)
    low[half:, :half] = off_t.astype(BF16)
    low[half:, half:] = jnp.where(small_row == small_col, -slope_second, second).astype(BF16)
    slopes = jnp.concatenate([slope_first, slope_second], axis=0)
    slopes = jnp.broadcast_to(slopes, (members, 128)).reshape(groups, rows, 128)
    lines[...] = slopes
    total_first = jnp.sum(first + off, axis=1, keepdims=True)
    total_second = jnp.sum(second + off_t, axis=1, keepdims=True)
    groups_half = groups // 2
    totals[:groups_half] = jnp.broadcast_to(total_first, (half, 128)).reshape(groups_half, rows, 128)
    totals[groups_half:] = jnp.broadcast_to(total_second, (half, 128)).reshape(
        groups_half, rows, 128
    )

    def weigh(i, top):
        at = chunk_at(i)
        block = gathered[:, :, at].reshape(members, CHUNK)
        rest = jnp.dot(low[...], block, preferred_element_type=F32)
        weighted[:, :, at] = rest.reshape(groups, rows, CHUNK)
        rest = jnp.abs(rest)
        for k in range(CHUNK // 128):
            top = jnp.maximum(top, rest[:, k * 128:(k + 1) * 128])
        return top

    share_rows = rows // 2
    lane = lax.broadcasted_iota(jnp.int32, (groups, share_rows, TILE), 2)

    def give(message, base, size, d):
        other, device = group_peer(d)
        at = message * groups + d
        span = pl.ds(base, size)
        return remote(
            sent.at[other, :, span], got.at[me, :, span], r_send.at[at], r_recv.at[at], device
        )

    sizes = []
    start, base, message = 0, 0, 0
    for parts in RETURN:
        first_step, last_step = start * steps, (start + sum(parts)) * steps
        top = lax.fori_loop(first_step, last_step, weigh, jnp.zeros((members, 128), F32))
        top = jnp.max(top, axis=1, keepdims=True)
        scale = jnp.maximum(top * 1.0079, 1e-30).astype(BF16).astype(F32)
        scale = jnp.broadcast_to(scale, (members, 128)).reshape(groups, rows, 128)
        inverses[...] = RANGE / scale
        heads = jnp.where(lane < 32, scale[:, :share_rows], slopes[:, :share_rows])
        tails = jnp.where(lane < 96, scale[:, share_rows:], slopes[:, share_rows:])
        sent[:, :, base:base + TILE] = jnp.where(lane < 64, heads, tails).astype(BF16)
        first_size = TILE + 2 * parts[0] * unit

        def encode(d):
            other = group_peer(d)[0]
            inverse = inverses[other]
            place_at, step_at = base + TILE, first_step
            for eighths in parts:
                width = eighths * unit

                def code(i, _, place_at=place_at, step_at=step_at, width=width):
                    rest = weighted[other, :, chunk_at(i + step_at)]
                    size = jnp.exp2(jnp.abs(rest) * wide(inverse) - SHIFT)
                    coded = jnp.where(rest < 0.0, -size, size).astype(BF16)
                    early = pl.ds(pl.multiple_of(place_at + i * CHUNK, 128), CHUNK)
                    late = pl.ds(pl.multiple_of(place_at + width + i * CHUNK, 128), CHUNK)
                    sent[other, :, early] = coded[:share_rows]
                    sent[other, :, late] = coded[share_rows:]
                    return 0

                lax.fori_loop(0, eighths * steps, code, 0)
                place_at, step_at = place_at + 2 * width, step_at + eighths * steps
            give(message, base, first_size, d).start()

        loop(groups, encode)
        sizes.append((base, first_size))
        base += first_size
        message += 1
        for eighths in parts[1:]:
            size = 2 * eighths * unit
            each(groups, lambda d: give(message, base, size, d).start())
            sizes.append((base, size))
            base += size
            message += 1
        start += sum(parts)

    each(chips, lambda d: obs_copy(d).wait_recv())
    obs = jnp.sqrt(jnp.sum(jnp.sum(obs_in[:chips], axis=0), axis=1, keepdims=True))
    near = jnp.broadcast_to(factor / obs, (rows, 128))
    share_factor = factor / members
    row_total = totals[me]

    def finish(piece, offset, count, along_own, value_at):
        def one(i, _):
            point = pl.ds(pl.multiple_of(piece * cols + offset + i * CHUNK, CHUNK), CHUNK)
            ours = own[:, point].astype(F32) * wide(along_own)
            out[:, point] = ours - analysis[:, point] * wide(near) + value_at(i)
            return 0

        lax.fori_loop(0, count, one, 0)

    finish(
        me, 0, cols // CHUNK, near - (row_total - lines[me]) * share_factor,
        lambda i: weighted[me, :, chunk_at(i)] * share_factor,
    )
    start, base, message = 0, 0, 0
    for parts in RETURN:
        tile_at = base
        base += TILE
        for eighths in parts:
            width = eighths * unit
            def take(d):
                give(message, *sizes[message], d).wait_recv()
                piece = group_source(d)
                tile = got[piece, :, tile_at:tile_at + TILE].astype(F32)
                scale = jnp.concatenate([tile[:, :1], tile[:, 64:65]], axis=0)
                scale = jnp.broadcast_to(scale * (share_factor / (RANGE * LN2)), (rows, 128))
                slope = jnp.concatenate([tile[:, 32:33], tile[:, 96:97]], axis=0)
                slope = jnp.broadcast_to(slope, (rows, 128))

                def decode(i):
                    early = pl.ds(pl.multiple_of(base + i * CHUNK, 128), CHUNK)
                    late = pl.ds(pl.multiple_of(base + width + i * CHUNK, 128), CHUNK)
                    coded = jnp.concatenate([got[piece, :, early], got[piece, :, late]], axis=0)
                    coded = coded.astype(F32)
                    size = (jnp.log(jnp.abs(coded)) + SHIFT * LN2) * wide(scale)
                    return jnp.where(coded < 0.0, -size, size)

                finish(
                    piece, start * unit, eighths * steps,
                    near - (row_total - slope) * share_factor, decode,
                )

            loop(groups, take)
            base += 2 * width
            start += eighths
            message += 1

    start = 0
    for index, eighths in enumerate(SPREAD):
        each(groups, lambda d: spread(index, start, d).wait_send())
        start += eighths
    each(chips, lambda d: obs_copy(d).wait_send())
    each(teams, lambda d: part_copy(d).wait_send())
    each(chips, lambda d: chip_copy(d).wait_send())
    each(teams, lambda d: sum_copy(d).wait_send())
    for message, (base, size) in enumerate(sizes):
        each(groups, lambda d: give(message, base, size, d).wait_send())


def on_device(ensemble, analysis):
    rows, points = ensemble.shape
    groups = lax.axis_size("member")
    places = lax.axis_size("space")
    chips = places // 2
    teams = groups * 2
    members = rows * groups
    cols = points // groups
    half = members // 2
    share = members // teams
    factor = math.sqrt(points * places)
    messages = sum(len(parts) for parts in RETURN)
    dma = pltpu.SemaphoreType.DMA
    return pl.pallas_call(
        functools.partial(kernel, groups, chips, factor),
        out_shape=pltpu.VMEM((rows, points), F32),
        in_specs=[pl.BlockSpec(memory_space=pltpu.HBM)] * 2,
        out_specs=pl.BlockSpec(memory_space=pltpu.VMEM),
        scratch_shapes=[
            pltpu.VMEM((groups, rows, cols), BF16),
            pltpu.VMEM((rows, points), BF16),
            pltpu.VMEM((1, points), F32),
            pltpu.VMEM((groups, rows, cols), F32),
            pltpu.VMEM((groups, rows // 2, 2 * cols + len(RETURN) * TILE), BF16),
            pltpu.VMEM((groups, rows // 2, 2 * cols + len(RETURN) * TILE), BF16),
            pltpu.VMEM((members, members), F32),
            pltpu.VMEM((teams, share, half), F32),
            pltpu.VMEM((teams, share, half), F32),
            pltpu.VMEM((chips, share, half), F32),
            pltpu.VMEM((teams, share, half), F32),
            pltpu.VMEM((members, members), BF16),
            pltpu.VMEM((groups, rows, 128), F32),
            pltpu.VMEM((groups, rows, 128), F32),
            pltpu.VMEM((groups, rows, 128), F32),
            pltpu.VMEM((chips + 2, rows, 128), F32),
            dma((len(SPREAD) * groups,)), dma((len(SPREAD) * groups,)),
            dma((teams,)), dma((teams,)),
            dma((chips,)), dma((chips,)),
            dma((teams,)), dma((teams,)),
            dma((messages * groups,)), dma((messages * groups,)),
            dma((chips,)), dma((chips,)),
            dma((3,)),
        ],
        compiler_params=pltpu.CompilerParams(
            collective_id=0, has_side_effects=True, vmem_limit_bytes=56 * 2**20
        ),
        cost_estimate=pl.CostEstimate(
            flops=4 * members * members * cols, bytes_accessed=8 * rows * points, transcendentals=0
        ),
    )(ensemble, analysis.reshape(1, points))


def solution(mesh):
    placed = (P("member", "space"), P("space"))
    return jax.shard_map(
        on_device, mesh=mesh, in_specs=placed, out_specs=P("member", "space"), check_vma=False
    )
```

```python
import functools
import math

import jax
import jax.numpy as jnp
from jax import lax
from jax.experimental import pallas as pl
from jax.experimental.pallas import tpu as pltpu
from jax.sharding import PartitionSpec as P

MESH = pl.DeviceIdType.MESH
F32 = jnp.float32
BF16 = jnp.bfloat16
RANGE = 125.0
LN2 = math.log(2.0)
CHUNK = 512
SPREAD = (2, 2, 2, 2)
RETURN = ((1,), (2, 2, 2, 1))
TILE = 128


def chunk_at(index):
    return pl.ds(pl.multiple_of(index * CHUNK, CHUNK), CHUNK)


def wide(tile):
    return jnp.concatenate([tile] * (CHUNK // 128), axis=1)


def kernel(
    groups, chips, factor, x_hbm, a_hbm, out,
    gathered, own, analysis, weighted, sent, got,
    products, part, part_in, chip_in, summed, low, totals, lines, inverses, obs_in,
    x_send, x_recv, p_send, p_recv, c_send, c_recv, s_send, s_recv, r_send, r_recv,
    o_send, o_recv, local_sem,
):
    me = lax.axis_index("member")
    place = lax.axis_index("space")
    core = lax.rem(place, 2)
    chip = place // 2
    rank = me * 2 + core
    teams = groups * 2
    rows = own.shape[0]
    cols = gathered.shape[2]
    members = groups * rows
    unit = cols // 8
    steps = unit // CHUNK

    def each(count, body):
        for d in range(1, count):
            body(d)

    def loop(count, body):
        lax.fori_loop(1, count, lambda d, _: (body(d), 0)[1], 0)

    def columns(index):
        return pl.ds(pl.multiple_of(index * cols, cols), cols)

    def group_peer(d):
        other = lax.rem(me // 2 + 2 * groups - d, groups // 2) * 2 + lax.rem(me + (groups - d) // (groups // 2), 2)
        return other, (other, place)

    def group_source(d):
        return lax.rem(me // 2 + d, groups // 2) * 2 + lax.rem(me + (groups - d) // (groups // 2), 2)

    def team_peer(d):
        other = lax.rem(rank + d, teams)
        return other, (other // 2, chip * 2 + lax.rem(other, 2))

    def chip_peer(d):
        other = lax.rem(chip + d, chips)
        return other, (me, other * 2 + core)

    sibling = (me, chip * 2 + 1 - core)

    def remote(src, dst, send, recv, device):
        return pltpu.make_async_remote_copy(
            src_ref=src, dst_ref=dst, send_sem=send, recv_sem=recv,
            device_id=device, device_id_type=MESH,
        )

    barrier = pltpu.get_barrier_semaphore()

    def greet(device):
        pl.semaphore_signal(barrier, inc=1, device_id=device, device_id_type=MESH)

    greet(sibling)
    each(groups, lambda d: greet(group_peer(d)[1]))
    each(chips, lambda d: greet(chip_peer(d)[1]))

    load_analysis = pltpu.make_async_copy(a_hbm, analysis, local_sem.at[0])
    load_analysis.start()
    load_own = pltpu.make_async_copy(x_hbm, own, local_sem.at[1])
    load_own.start()
    keep = pltpu.make_async_copy(x_hbm.at[:, columns(me)], gathered.at[me], local_sem.at[2])
    keep.start()

    pl.semaphore_wait(barrier, groups + chips - 1)

    def spread(index, start, d):
        width = SPREAD[index] * unit
        other, device = group_peer(d)
        src = pl.ds(pl.multiple_of(other * cols + start * unit, unit), width)
        at = index * groups + d
        return remote(
            x_hbm.at[:, src], gathered.at[me, :, pl.ds(start * unit, width)],
            x_send.at[at], x_recv.at[at], device,
        )

    start = 0
    for index, eighths in enumerate(SPREAD):
        each(groups, lambda d: spread(index, start, d).start())
        start += eighths

    load_analysis.wait()
    load_own.wait()

    def add_distance(i, total):
        at = chunk_at(i)
        deviation = own[:, at].astype(F32) - analysis[:, at]
        square = deviation * deviation
        for k in range(CHUNK // 128):
            total = total + square[:, k * 128:(k + 1) * 128]
        return total

    distance = lax.fori_loop(0, own.shape[1] // CHUNK, add_distance, jnp.zeros((rows, 128), F32))
    obs_in[chips] = distance
    pair = remote(obs_in.at[chips], obs_in.at[chips + 1], o_send.at[0], o_recv.at[0], sibling)
    pair.start()
    pair.wait()
    obs_in[chip] = distance + obs_in[chips + 1]

    def obs_copy(d):
        return remote(
            obs_in.at[chip], obs_in.at[chip], o_send.at[d], o_recv.at[d], chip_peer(d)[1]
        )

    each(chips, lambda d: obs_copy(d).start())
    keep.wait()

    def products_of(start, size):
        block = gathered[:, :, start:start + size].reshape(members, size)
        return lax.dot_general(block, block, (((1,), (1,)), ((), ())), preferred_element_type=F32)

    start = 0
    for index, eighths in enumerate(SPREAD):
        each(groups, lambda d: spread(index, start, d).wait_recv())
        if start:
            products[...] += products_of(start * unit, eighths * unit)
        else:
            products[...] = products_of(0, eighths * unit)
        start += eighths
    cross = products[...]
    row_index = lax.broadcasted_iota(jnp.int32, (members, members), 0)
    col_index = lax.broadcasted_iota(jnp.int32, (members, members), 1)
    diagonal = jnp.where(row_index == col_index, cross, 0.0)
    norm_rows = jnp.sum(diagonal, axis=1, keepdims=True)
    norm_cols = jnp.sum(diagonal, axis=0, keepdims=True)
    pair_sq = norm_rows + norm_cols - 2.0 * cross
    half = members // 2
    small_row = lax.broadcasted_iota(jnp.int32, (half, half), 0)
    small_col = lax.broadcasted_iota(jnp.int32, (half, half), 1)
    upper = small_col > small_row
    lower = small_col < small_row
    share = members // teams
    part[: teams // 2] = pair_sq[:half, half:].reshape(teams // 2, share, half)
    part[teams // 2 :] = jnp.where(upper, pair_sq[:half, :half], pair_sq[half:, half:]).reshape(
        teams // 2, share, half
    )

    def part_copy(d):
        other, device = team_peer(d)
        return remote(part.at[other], part_in.at[rank], p_send.at[d], p_recv.at[d], device)

    def chip_copy(d):
        return remote(
            chip_in.at[chip], chip_in.at[chip], c_send.at[d], c_recv.at[d], chip_peer(d)[1]
        )

    def sum_copy(d):
        return remote(
            summed.at[rank], summed.at[rank], s_send.at[d], s_recv.at[d], team_peer(d)[1]
        )

    each(teams, lambda d: part_copy(d).start())
    part_in[rank] = part[rank]
    each(teams, lambda d: part_copy(d).wait_recv())
    chip_in[chip] = jnp.sum(part_in[...], axis=0)
    each(chips, lambda d: chip_copy(d).start())
    each(chips, lambda d: chip_copy(d).wait_recv())
    summed[rank] = jnp.sum(chip_in[...], axis=0)
    each(teams, lambda d: sum_copy(d).start())
    each(teams, lambda d: sum_copy(d).wait_recv())

    off = 1.0 / jnp.sqrt(summed[: teams // 2].reshape(half, half))
    triangles = summed[teams // 2 :].reshape(half, half)
    triangles = jnp.where(small_row == small_col, 1.0, triangles)
    triangles = 1.0 / jnp.sqrt(triangles)
    above = jnp.where(upper, triangles, 0.0)
    below = jnp.where(lower, triangles, 0.0)
    first = above + above.T
    second = below + below.T
    off_t = off.T
    def slope_of(own_part, own_products, cross_part, cross_products):
        along = jnp.sum(own_part * own_products + cross_part * cross_products, axis=1, keepdims=True)
        square = jnp.sum(jnp.where(small_row == small_col, own_products, 0.0), axis=1, keepdims=True)
        slope = jnp.where(square > 0.0, along / jnp.where(square > 0.0, square, 1.0), 0.0)
        return slope.astype(BF16).astype(F32)

    slope_first = slope_of(first, products[:half, :half], off, products[:half, half:])
    slope_second = slope_of(second, products[half:, half:], off_t, products[half:, :half])
    low[:half, :half] = jnp.where(small_row == small_col, -slope_first, first).astype(BF16)
    low[:half, half:] = off.astype(BF16)
    low[half:, :half] = off_t.astype(BF16)
    low[half:, half:] = jnp.where(small_row == small_col, -slope_second, second).astype(BF16)
    slopes = jnp.concatenate([slope_first, slope_second], axis=0)
    slopes = jnp.broadcast_to(slopes, (members, 128)).reshape(groups, rows, 128)
    lines[...] = slopes
    total_first = jnp.sum(first + off, axis=1, keepdims=True)
    total_second = jnp.sum(second + off_t, axis=1, keepdims=True)
    groups_half = groups // 2
    totals[:groups_half] = jnp.broadcast_to(total_first, (half, 128)).reshape(groups_half, rows, 128)
    totals[groups_half:] = jnp.broadcast_to(total_second, (half, 128)).reshape(
        groups_half, rows, 128
    )

    def weigh(i, top):
        at = chunk_at(i)
        block = gathered[:, :, at].reshape(members, CHUNK)
        rest = jnp.dot(low[...], block, preferred_element_type=F32)
        weighted[:, :, at] = rest.reshape(groups, rows, CHUNK)
        rest = jnp.abs(rest)
        for k in range(CHUNK // 128):
            top = jnp.maximum(top, rest[:, k * 128:(k + 1) * 128])
        return top

    share_rows = rows // 2
    lane = lax.broadcasted_iota(jnp.int32, (groups, share_rows, TILE), 2)

    def give(message, base, size, d):
        other, device = group_peer(d)
        at = message * groups + d
        span = pl.ds(base, size)
        return remote(
            sent.at[other, :, span], got.at[me, :, span], r_send.at[at], r_recv.at[at], device
        )

    sizes = []
    start, base, message = 0, 0, 0
    for parts in RETURN:
        first_step, last_step = start * steps, (start + sum(parts)) * steps
        top = lax.fori_loop(first_step, last_step, weigh, jnp.zeros((members, 128), F32))
        top = jnp.max(top, axis=1, keepdims=True)
        scale = jnp.maximum(top * 1.0079, 1e-30).astype(BF16).astype(F32)
        scale = jnp.broadcast_to(scale, (members, 128)).reshape(groups, rows, 128)
        inverses[...] = RANGE / scale
        heads = jnp.where(lane < 32, scale[:, :share_rows], slopes[:, :share_rows])
        tails = jnp.where(lane < 96, scale[:, share_rows:], slopes[:, share_rows:])
        sent[:, :, base:base + TILE] = jnp.where(lane < 64, heads, tails).astype(BF16)
        first_size = TILE + 2 * parts[0] * unit

        def encode(d):
            other = group_peer(d)[0]
            inverse = inverses[other]
            place_at, step_at = base + TILE, first_step
            for eighths in parts:
                width = eighths * unit

                def code(i, _, place_at=place_at, step_at=step_at, width=width):
                    rest = weighted[other, :, chunk_at(i + step_at)]
                    coded = jnp.exp2(rest * wide(inverse)).astype(BF16)
                    early = pl.ds(pl.multiple_of(place_at + i * CHUNK, 128), CHUNK)
                    late = pl.ds(pl.multiple_of(place_at + width + i * CHUNK, 128), CHUNK)
                    sent[other, :, early] = coded[:share_rows]
                    sent[other, :, late] = coded[share_rows:]
                    return 0

                lax.fori_loop(0, eighths * steps, code, 0)
                place_at, step_at = place_at + 2 * width, step_at + eighths * steps
            give(message, base, first_size, d).start()

        loop(groups, encode)
        sizes.append((base, first_size))
        base += first_size
        message += 1
        for eighths in parts[1:]:
            size = 2 * eighths * unit
            each(groups, lambda d: give(message, base, size, d).start())
            sizes.append((base, size))
            base += size
            message += 1
        start += sum(parts)

    each(chips, lambda d: obs_copy(d).wait_recv())
    obs = jnp.sqrt(jnp.sum(jnp.sum(obs_in[:chips], axis=0), axis=1, keepdims=True))
    near = jnp.broadcast_to(factor / obs, (rows, 128))
    share_factor = factor / members
    row_total = totals[me]

    def finish(piece, offset, count, along_own, value_at):
        def one(i, _):
            point = pl.ds(pl.multiple_of(piece * cols + offset + i * CHUNK, CHUNK), CHUNK)
            ours = own[:, point].astype(F32) * wide(along_own)
            out[:, point] = ours - analysis[:, point] * wide(near) + value_at(i)
            return 0

        lax.fori_loop(0, count, one, 0)

    finish(
        me, 0, cols // CHUNK, near - (row_total - lines[me]) * share_factor,
        lambda i: weighted[me, :, chunk_at(i)] * share_factor,
    )
    start, base, message = 0, 0, 0
    for parts in RETURN:
        tile_at = base
        base += TILE
        for eighths in parts:
            width = eighths * unit
            def take(d):
                give(message, *sizes[message], d).wait_recv()
                piece = group_source(d)
                tile = got[piece, :, tile_at:tile_at + TILE].astype(F32)
                scale = jnp.concatenate([tile[:, :1], tile[:, 64:65]], axis=0)
                scale = jnp.broadcast_to(scale * (share_factor / (RANGE * LN2)), (rows, 128))
                slope = jnp.concatenate([tile[:, 32:33], tile[:, 96:97]], axis=0)
                slope = jnp.broadcast_to(slope, (rows, 128))

                def decode(i):
                    early = pl.ds(pl.multiple_of(base + i * CHUNK, 128), CHUNK)
                    late = pl.ds(pl.multiple_of(base + width + i * CHUNK, 128), CHUNK)
                    coded = jnp.concatenate([got[piece, :, early], got[piece, :, late]], axis=0)
                    return jnp.log(coded.astype(F32)) * wide(scale)

                finish(
                    piece, start * unit, eighths * steps,
                    near - (row_total - slope) * share_factor, decode,
                )

            loop(groups, take)
            base += 2 * width
            start += eighths
            message += 1

    start = 0
    for index, eighths in enumerate(SPREAD):
        each(groups, lambda d: spread(index, start, d).wait_send())
        start += eighths
    each(chips, lambda d: obs_copy(d).wait_send())
    each(teams, lambda d: part_copy(d).wait_send())
    each(chips, lambda d: chip_copy(d).wait_send())
    each(teams, lambda d: sum_copy(d).wait_send())
    for message, (base, size) in enumerate(sizes):
        each(groups, lambda d: give(message, base, size, d).wait_send())


def on_device(ensemble, analysis):
    rows, points = ensemble.shape
    groups = lax.axis_size("member")
    places = lax.axis_size("space")
    chips = places // 2
    teams = groups * 2
    members = rows * groups
    cols = points // groups
    half = members // 2
    share = members // teams
    factor = math.sqrt(points * places)
    messages = sum(len(parts) for parts in RETURN)
    dma = pltpu.SemaphoreType.DMA
    return pl.pallas_call(
        functools.partial(kernel, groups, chips, factor),
        out_shape=pltpu.VMEM((rows, points), F32),
        in_specs=[pl.BlockSpec(memory_space=pltpu.HBM)] * 2,
        out_specs=pl.BlockSpec(memory_space=pltpu.VMEM),
        scratch_shapes=[
            pltpu.VMEM((groups, rows, cols), BF16),
            pltpu.VMEM((rows, points), BF16),
            pltpu.VMEM((1, points), F32),
            pltpu.VMEM((groups, rows, cols), F32),
            pltpu.VMEM((groups, rows // 2, 2 * cols + len(RETURN) * TILE), BF16),
            pltpu.VMEM((groups, rows // 2, 2 * cols + len(RETURN) * TILE), BF16),
            pltpu.VMEM((members, members), F32),
            pltpu.VMEM((teams, share, half), F32),
            pltpu.VMEM((teams, share, half), F32),
            pltpu.VMEM((chips, share, half), F32),
            pltpu.VMEM((teams, share, half), F32),
            pltpu.VMEM((members, members), BF16),
            pltpu.VMEM((groups, rows, 128), F32),
            pltpu.VMEM((groups, rows, 128), F32),
            pltpu.VMEM((groups, rows, 128), F32),
            pltpu.VMEM((chips + 2, rows, 128), F32),
            dma((len(SPREAD) * groups,)), dma((len(SPREAD) * groups,)),
            dma((teams,)), dma((teams,)),
            dma((chips,)), dma((chips,)),
            dma((teams,)), dma((teams,)),
            dma((messages * groups,)), dma((messages * groups,)),
            dma((chips,)), dma((chips,)),
            dma((3,)),
        ],
        compiler_params=pltpu.CompilerParams(
            collective_id=0, has_side_effects=True, vmem_limit_bytes=56 * 2**20
        ),
        cost_estimate=pl.CostEstimate(
            flops=4 * members * members * cols, bytes_accessed=8 * rows * points, transcendentals=0
        ),
    )(ensemble, analysis.reshape(1, points))


def solution(mesh):
    placed = (P("member", "space"), P("space"))
    return jax.shard_map(
        on_device, mesh=mesh, in_specs=placed, out_specs=P("member", "space"), check_vma=False
    )
```

```python
import functools
import math

import jax
import jax.numpy as jnp
from jax import lax
from jax.experimental import pallas as pl
from jax.experimental.pallas import tpu as pltpu
from jax.sharding import PartitionSpec as P

MESH = pl.DeviceIdType.MESH
F32 = jnp.float32
BF16 = jnp.bfloat16
RANGE = 125.0
LN2 = math.log(2.0)
CHUNK = 512
SPREAD = (2, 2, 2, 2)
RETURN = ((1,), (2, 2, 2, 1))
TILE = 128
CHIP_STEPS = ((2, 1), (1, 1), (3, 1), (2, 0), (0, 1), (1, 0), (3, 0))
STEPS = ((2, 1), (2, 0), (3, 1), (1, 1), (0, 1), (3, 0), (1, 0))


def chunk_at(index):
    return pl.ds(pl.multiple_of(index * CHUNK, CHUNK), CHUNK)


def wide(tile):
    return jnp.concatenate([tile] * (CHUNK // 128), axis=1)


def kernel(
    groups, chips, factor, x_hbm, a_hbm, out,
    gathered, own, analysis, weighted, sent, got,
    products, part, part_in, chip_in, summed, low, totals, lines, inverses, obs_in,
    x_send, x_recv, p_send, p_recv, c_send, c_recv, s_send, s_recv, r_send, r_recv,
    o_send, o_recv, local_sem,
):
    me = lax.axis_index("member")
    place = lax.axis_index("space")
    core = lax.rem(place, 2)
    chip = place // 2
    rank = me * 2 + core
    teams = groups * 2
    rows = own.shape[0]
    cols = gathered.shape[2]
    members = groups * rows
    unit = cols // 8
    steps = unit // CHUNK

    def each(count, body):
        for d in range(1, count):
            body(d)

    def columns(index):
        return pl.ds(pl.multiple_of(index * cols, cols), cols)

    def group_peer(d):
        dz, dy = STEPS[d - 1]
        other = lax.rem(me // 2 + dz, groups // 2) * 2 + lax.rem(me + dy, 2)
        return other, (other, place)

    def group_source(d):
        dz, dy = STEPS[d - 1]
        return lax.rem(me // 2 + groups // 2 - dz, groups // 2) * 2 + lax.rem(me + dy, 2)

    def team_peer(d):
        member = group_peer((d + 1) // 2)[0] if d < teams - 1 else me
        its_core = core if d % 2 == 0 else 1 - core
        return member * 2 + its_core, (member, chip * 2 + its_core)

    def chip_peer(d):
        dx, dy = CHIP_STEPS[d - 1]
        other = lax.rem(chip // 2 + dx, chips // 2) * 2 + lax.rem(chip + dy, 2)
        return other, (me, other * 2 + core)

    sibling = (me, chip * 2 + 1 - core)

    def remote(src, dst, send, recv, device):
        return pltpu.make_async_remote_copy(
            src_ref=src, dst_ref=dst, send_sem=send, recv_sem=recv,
            device_id=device, device_id_type=MESH,
        )

    barrier = pltpu.get_barrier_semaphore()

    def greet(device):
        pl.semaphore_signal(barrier, inc=1, device_id=device, device_id_type=MESH)

    greet(sibling)
    each(groups, lambda d: greet(group_peer(d)[1]))
    each(chips, lambda d: greet(chip_peer(d)[1]))

    load_analysis = pltpu.make_async_copy(a_hbm, analysis, local_sem.at[0])
    load_analysis.start()
    load_own = pltpu.make_async_copy(x_hbm, own, local_sem.at[1])
    load_own.start()
    keep = pltpu.make_async_copy(x_hbm.at[:, columns(me)], gathered.at[me], local_sem.at[2])
    keep.start()

    pl.semaphore_wait(barrier, groups + chips - 1)

    def spread(index, start, d):
        width = SPREAD[index] * unit
        other, device = group_peer(d)
        src = pl.ds(pl.multiple_of(other * cols + start * unit, unit), width)
        at = index * groups + d
        return remote(
            x_hbm.at[:, src], gathered.at[me, :, pl.ds(start * unit, width)],
            x_send.at[at], x_recv.at[at], device,
        )

    start = 0
    for index, eighths in enumerate(SPREAD):
        each(groups, lambda d: spread(index, start, d).start())
        start += eighths

    load_analysis.wait()
    load_own.wait()

    def add_distance(i, total):
        at = chunk_at(i)
        deviation = own[:, at].astype(F32) - analysis[:, at]
        square = deviation * deviation
        for k in range(CHUNK // 128):
            total = total + square[:, k * 128:(k + 1) * 128]
        return total

    distance = lax.fori_loop(0, own.shape[1] // CHUNK, add_distance, jnp.zeros((rows, 128), F32))
    obs_in[chips] = distance
    pair = remote(obs_in.at[chips], obs_in.at[chips + 1], o_send.at[0], o_recv.at[0], sibling)
    pair.start()
    pair.wait()
    obs_in[chip] = distance + obs_in[chips + 1]

    def obs_copy(d):
        return remote(
            obs_in.at[chip], obs_in.at[chip], o_send.at[d], o_recv.at[d], chip_peer(d)[1]
        )

    each(chips, lambda d: obs_copy(d).start())
    keep.wait()

    def products_of(start, size):
        block = gathered[:, :, start:start + size].reshape(members, size)
        return lax.dot_general(block, block, (((1,), (1,)), ((), ())), preferred_element_type=F32)

    start = 0
    for index, eighths in enumerate(SPREAD):
        each(groups, lambda d: spread(index, start, d).wait_recv())
        if start:
            products[...] += products_of(start * unit, eighths * unit)
        else:
            products[...] = products_of(0, eighths * unit)
        start += eighths
    cross = products[...]
    row_index = lax.broadcasted_iota(jnp.int32, (members, members), 0)
    col_index = lax.broadcasted_iota(jnp.int32, (members, members), 1)
    diagonal = jnp.where(row_index == col_index, cross, 0.0)
    norm_rows = jnp.sum(diagonal, axis=1, keepdims=True)
    norm_cols = jnp.sum(diagonal, axis=0, keepdims=True)
    pair_sq = norm_rows + norm_cols - 2.0 * cross
    half = members // 2
    small_row = lax.broadcasted_iota(jnp.int32, (half, half), 0)
    small_col = lax.broadcasted_iota(jnp.int32, (half, half), 1)
    upper = small_col > small_row
    lower = small_col < small_row
    share = members // teams
    part[: teams // 2] = pair_sq[:half, half:].reshape(teams // 2, share, half)
    part[teams // 2 :] = jnp.where(upper, pair_sq[:half, :half], pair_sq[half:, half:]).reshape(
        teams // 2, share, half
    )

    def part_copy(d):
        other, device = team_peer(d)
        return remote(part.at[other], part_in.at[rank], p_send.at[d], p_recv.at[d], device)

    def chip_copy(d):
        return remote(
            chip_in.at[chip], chip_in.at[chip], c_send.at[d], c_recv.at[d], chip_peer(d)[1]
        )

    def sum_copy(d):
        return remote(
            summed.at[rank], summed.at[rank], s_send.at[d], s_recv.at[d], team_peer(d)[1]
        )

    each(teams, lambda d: part_copy(d).start())
    part_in[rank] = part[rank]
    each(teams, lambda d: part_copy(d).wait_recv())
    chip_in[chip] = jnp.sum(part_in[...], axis=0)
    each(chips, lambda d: chip_copy(d).start())
    each(chips, lambda d: chip_copy(d).wait_recv())
    summed[rank] = jnp.sum(chip_in[...], axis=0)
    each(teams, lambda d: sum_copy(d).start())
    each(teams, lambda d: sum_copy(d).wait_recv())

    off = 1.0 / jnp.sqrt(summed[: teams // 2].reshape(half, half))
    triangles = summed[teams // 2 :].reshape(half, half)
    triangles = jnp.where(small_row == small_col, 1.0, triangles)
    triangles = 1.0 / jnp.sqrt(triangles)
    above = jnp.where(upper, triangles, 0.0)
    below = jnp.where(lower, triangles, 0.0)
    first = above + above.T
    second = below + below.T
    off_t = off.T
    def slope_of(own_part, own_products, cross_part, cross_products):
        along = jnp.sum(own_part * own_products + cross_part * cross_products, axis=1, keepdims=True)
        square = jnp.sum(jnp.where(small_row == small_col, own_products, 0.0), axis=1, keepdims=True)
        slope = jnp.where(square > 0.0, along / jnp.where(square > 0.0, square, 1.0), 0.0)
        return slope.astype(BF16).astype(F32)

    slope_first = slope_of(first, products[:half, :half], off, products[:half, half:])
    slope_second = slope_of(second, products[half:, half:], off_t, products[half:, :half])
    low[:half, :half] = jnp.where(small_row == small_col, -slope_first, first).astype(BF16)
    low[:half, half:] = off.astype(BF16)
    low[half:, :half] = off_t.astype(BF16)
    low[half:, half:] = jnp.where(small_row == small_col, -slope_second, second).astype(BF16)
    slopes = jnp.concatenate([slope_first, slope_second], axis=0)
    slopes = jnp.broadcast_to(slopes, (members, 128)).reshape(groups, rows, 128)
    lines[...] = slopes
    total_first = jnp.sum(first + off, axis=1, keepdims=True)
    total_second = jnp.sum(second + off_t, axis=1, keepdims=True)
    groups_half = groups // 2
    totals[:groups_half] = jnp.broadcast_to(total_first, (half, 128)).reshape(groups_half, rows, 128)
    totals[groups_half:] = jnp.broadcast_to(total_second, (half, 128)).reshape(
        groups_half, rows, 128
    )

    def weigh(i, top):
        at = chunk_at(i)
        block = gathered[:, :, at].reshape(members, CHUNK)
        rest = jnp.dot(low[...], block, preferred_element_type=F32)
        weighted[:, :, at] = rest.reshape(groups, rows, CHUNK)
        rest = jnp.abs(rest)
        for k in range(CHUNK // 128):
            top = jnp.maximum(top, rest[:, k * 128:(k + 1) * 128])
        return top

    share_rows = rows // 2
    lane = lax.broadcasted_iota(jnp.int32, (groups, share_rows, TILE), 2)

    def give(message, base, size, d):
        other, device = group_peer(d)
        at = message * groups + d
        span = pl.ds(base, size)
        return remote(
            sent.at[other, :, span], got.at[me, :, span], r_send.at[at], r_recv.at[at], device
        )

    sizes = []
    start, base, message = 0, 0, 0
    for parts in RETURN:
        first_step, last_step = start * steps, (start + sum(parts)) * steps
        top = lax.fori_loop(first_step, last_step, weigh, jnp.zeros((members, 128), F32))
        top = jnp.max(top, axis=1, keepdims=True)
        scale = jnp.maximum(top * 1.0079, 1e-30).astype(BF16).astype(F32)
        scale = jnp.broadcast_to(scale, (members, 128)).reshape(groups, rows, 128)
        inverses[...] = RANGE / scale
        heads = jnp.where(lane < 32, scale[:, :share_rows], slopes[:, :share_rows])
        tails = jnp.where(lane < 96, scale[:, share_rows:], slopes[:, share_rows:])
        sent[:, :, base:base + TILE] = jnp.where(lane < 64, heads, tails).astype(BF16)
        first_size = TILE + 2 * parts[0] * unit

        def encode(d):
            other = group_peer(d)[0]
            inverse = inverses[other]
            place_at, step_at = base + TILE, first_step
            for eighths in parts:
                width = eighths * unit

                def code(i, _, place_at=place_at, step_at=step_at, width=width):
                    rest = weighted[other, :, chunk_at(i + step_at)]
                    coded = jnp.exp2(rest * wide(inverse)).astype(BF16)
                    early = pl.ds(pl.multiple_of(place_at + i * CHUNK, 128), CHUNK)
                    late = pl.ds(pl.multiple_of(place_at + width + i * CHUNK, 128), CHUNK)
                    sent[other, :, early] = coded[:share_rows]
                    sent[other, :, late] = coded[share_rows:]
                    return 0

                lax.fori_loop(0, eighths * steps, code, 0)
                place_at, step_at = place_at + 2 * width, step_at + eighths * steps
            give(message, base, first_size, d).start()

        each(groups, encode)
        sizes.append((base, first_size))
        base += first_size
        message += 1
        for eighths in parts[1:]:
            size = 2 * eighths * unit
            each(groups, lambda d: give(message, base, size, d).start())
            sizes.append((base, size))
            base += size
            message += 1
        start += sum(parts)

    each(chips, lambda d: obs_copy(d).wait_recv())
    obs = jnp.sqrt(jnp.sum(jnp.sum(obs_in[:chips], axis=0), axis=1, keepdims=True))
    near = jnp.broadcast_to(factor / obs, (rows, 128))
    share_factor = factor / members
    row_total = totals[me]

    def finish(piece, offset, count, along_own, value_at):
        def one(i, _):
            point = pl.ds(pl.multiple_of(piece * cols + offset + i * CHUNK, CHUNK), CHUNK)
            ours = own[:, point].astype(F32) * wide(along_own)
            out[:, point] = ours - analysis[:, point] * wide(near) + value_at(i)
            return 0

        lax.fori_loop(0, count, one, 0)

    finish(
        me, 0, cols // CHUNK, near - (row_total - lines[me]) * share_factor,
        lambda i: weighted[me, :, chunk_at(i)] * share_factor,
    )
    start, base, message = 0, 0, 0
    for parts in RETURN:
        tile_at = base
        base += TILE
        for eighths in parts:
            width = eighths * unit
            def take(d):
                give(message, *sizes[message], d).wait_recv()
                piece = group_source(d)
                tile = got[piece, :, tile_at:tile_at + TILE].astype(F32)
                scale = jnp.concatenate([tile[:, :1], tile[:, 64:65]], axis=0)
                scale = jnp.broadcast_to(scale * (share_factor / (RANGE * LN2)), (rows, 128))
                slope = jnp.concatenate([tile[:, 32:33], tile[:, 96:97]], axis=0)
                slope = jnp.broadcast_to(slope, (rows, 128))

                def decode(i):
                    early = pl.ds(pl.multiple_of(base + i * CHUNK, 128), CHUNK)
                    late = pl.ds(pl.multiple_of(base + width + i * CHUNK, 128), CHUNK)
                    coded = jnp.concatenate([got[piece, :, early], got[piece, :, late]], axis=0)
                    return jnp.log(coded.astype(F32)) * wide(scale)

                finish(
                    piece, start * unit, eighths * steps,
                    near - (row_total - slope) * share_factor, decode,
                )

            each(groups, take)
            base += 2 * width
            start += eighths
            message += 1

    start = 0
    for index, eighths in enumerate(SPREAD):
        each(groups, lambda d: spread(index, start, d).wait_send())
        start += eighths
    each(chips, lambda d: obs_copy(d).wait_send())
    each(teams, lambda d: part_copy(d).wait_send())
    each(chips, lambda d: chip_copy(d).wait_send())
    each(teams, lambda d: sum_copy(d).wait_send())
    for message, (base, size) in enumerate(sizes):
        each(groups, lambda d: give(message, base, size, d).wait_send())


def on_device(ensemble, analysis):
    rows, points = ensemble.shape
    groups = lax.axis_size("member")
    places = lax.axis_size("space")
    chips = places // 2
    teams = groups * 2
    members = rows * groups
    cols = points // groups
    half = members // 2
    share = members // teams
    factor = math.sqrt(points * places)
    messages = sum(len(parts) for parts in RETURN)
    dma = pltpu.SemaphoreType.DMA
    return pl.pallas_call(
        functools.partial(kernel, groups, chips, factor),
        out_shape=pltpu.VMEM((rows, points), F32),
        in_specs=[pl.BlockSpec(memory_space=pltpu.HBM)] * 2,
        out_specs=pl.BlockSpec(memory_space=pltpu.VMEM),
        scratch_shapes=[
            pltpu.VMEM((groups, rows, cols), BF16),
            pltpu.VMEM((rows, points), BF16),
            pltpu.VMEM((1, points), F32),
            pltpu.VMEM((groups, rows, cols), F32),
            pltpu.VMEM((groups, rows // 2, 2 * cols + len(RETURN) * TILE), BF16),
            pltpu.VMEM((groups, rows // 2, 2 * cols + len(RETURN) * TILE), BF16),
            pltpu.VMEM((members, members), F32),
            pltpu.VMEM((teams, share, half), F32),
            pltpu.VMEM((teams, share, half), F32),
            pltpu.VMEM((chips, share, half), F32),
            pltpu.VMEM((teams, share, half), F32),
            pltpu.VMEM((members, members), BF16),
            pltpu.VMEM((groups, rows, 128), F32),
            pltpu.VMEM((groups, rows, 128), F32),
            pltpu.VMEM((groups, rows, 128), F32),
            pltpu.VMEM((chips + 2, rows, 128), F32),
            dma((len(SPREAD) * groups,)), dma((len(SPREAD) * groups,)),
            dma((teams,)), dma((teams,)),
            dma((chips,)), dma((chips,)),
            dma((teams,)), dma((teams,)),
            dma((messages * groups,)), dma((messages * groups,)),
            dma((chips,)), dma((chips,)),
            dma((3,)),
        ],
        compiler_params=pltpu.CompilerParams(
            collective_id=0, has_side_effects=True, vmem_limit_bytes=56 * 2**20
        ),
        cost_estimate=pl.CostEstimate(
            flops=4 * members * members * cols, bytes_accessed=8 * rows * points, transcendentals=0
        ),
    )(ensemble, analysis.reshape(1, points))


def solution(mesh):
    placed = (P("member", "space"), P("space"))
    return jax.shard_map(
        on_device, mesh=mesh, in_specs=placed, out_specs=P("member", "space"), check_vma=False
    )
```

```python
import functools
import math

import jax
import jax.numpy as jnp
from jax import lax
from jax.experimental import pallas as pl
from jax.experimental.pallas import tpu as pltpu
from jax.sharding import PartitionSpec as P

MESH = pl.DeviceIdType.MESH
F32 = jnp.float32
BF16 = jnp.bfloat16
RANGE = 125.0
LN2 = math.log(2.0)
CHUNK = 512
SPREAD = (3, 3, 2)
RETURN = ((1,), (4, 2, 1))
TILE = 128
CHIP_STEPS = ((2, 1), (1, 1), (3, 1), (2, 0), (0, 1), (1, 0), (3, 0))
STEPS = ((2, 1), (2, 0), (3, 1), (1, 1), (0, 1), (3, 0), (1, 0))


def chunk_at(index):
    return pl.ds(pl.multiple_of(index * CHUNK, CHUNK), CHUNK)


def wide(tile):
    return jnp.concatenate([tile] * (CHUNK // 128), axis=1)


def kernel(
    groups, chips, factor, x_hbm, a_hbm, out,
    gathered, own, analysis, weighted, sent, got,
    products, part, part_in, chip_in, summed, low, totals, lines, inverses, obs_in,
    x_send, x_recv, p_send, p_recv, c_send, c_recv, s_send, s_recv, r_send, r_recv,
    o_send, o_recv, local_sem,
):
    me = lax.axis_index("member")
    place = lax.axis_index("space")
    core = lax.rem(place, 2)
    chip = place // 2
    rank = me * 2 + core
    teams = groups * 2
    rows = own.shape[0]
    cols = gathered.shape[2]
    members = groups * rows
    unit = cols // 8
    steps = unit // CHUNK

    def each(count, body):
        for d in range(1, count):
            body(d)

    def columns(index):
        return pl.ds(pl.multiple_of(index * cols, cols), cols)

    def group_peer(d):
        dz, dy = STEPS[d - 1]
        other = lax.rem(me // 2 + dz, groups // 2) * 2 + lax.rem(me + dy, 2)
        return other, (other, place)

    def group_source(d):
        dz, dy = STEPS[d - 1]
        return lax.rem(me // 2 + groups // 2 - dz, groups // 2) * 2 + lax.rem(me + dy, 2)

    def team_peer(d):
        member = group_peer((d + 1) // 2)[0] if d < teams - 1 else me
        its_core = core if d % 2 == 0 else 1 - core
        return member * 2 + its_core, (member, chip * 2 + its_core)

    def chip_peer(d):
        dx, dy = CHIP_STEPS[d - 1]
        other = lax.rem(chip // 2 + dx, chips // 2) * 2 + lax.rem(chip + dy, 2)
        return other, (me, other * 2 + core)

    sibling = (me, chip * 2 + 1 - core)

    def remote(src, dst, send, recv, device):
        return pltpu.make_async_remote_copy(
            src_ref=src, dst_ref=dst, send_sem=send, recv_sem=recv,
            device_id=device, device_id_type=MESH,
        )

    barrier = pltpu.get_barrier_semaphore()

    def greet(device):
        pl.semaphore_signal(barrier, inc=1, device_id=device, device_id_type=MESH)

    greet(sibling)
    each(groups, lambda d: greet(group_peer(d)[1]))
    each(chips, lambda d: greet(chip_peer(d)[1]))

    load_analysis = pltpu.make_async_copy(a_hbm, analysis, local_sem.at[0])
    load_analysis.start()
    load_own = pltpu.make_async_copy(x_hbm, own, local_sem.at[1])
    load_own.start()
    keep = pltpu.make_async_copy(x_hbm.at[:, columns(me)], gathered.at[me], local_sem.at[2])
    keep.start()

    pl.semaphore_wait(barrier, groups + chips - 1)

    def spread(index, start, d):
        width = SPREAD[index] * unit
        other, device = group_peer(d)
        src = pl.ds(pl.multiple_of(other * cols + start * unit, unit), width)
        at = index * groups + d
        return remote(
            x_hbm.at[:, src], gathered.at[me, :, pl.ds(start * unit, width)],
            x_send.at[at], x_recv.at[at], device,
        )

    start = 0
    for index, eighths in enumerate(SPREAD):
        each(groups, lambda d: spread(index, start, d).start())
        start += eighths

    load_analysis.wait()
    load_own.wait()

    def add_distance(i, total):
        at = chunk_at(i)
        deviation = own[:, at].astype(F32) - analysis[:, at]
        square = deviation * deviation
        for k in range(CHUNK // 128):
            total = total + square[:, k * 128:(k + 1) * 128]
        return total

    distance = lax.fori_loop(0, own.shape[1] // CHUNK, add_distance, jnp.zeros((rows, 128), F32))
    obs_in[chips] = distance
    pair = remote(obs_in.at[chips], obs_in.at[chips + 1], o_send.at[0], o_recv.at[0], sibling)
    pair.start()
    pair.wait()
    obs_in[chip] = distance + obs_in[chips + 1]

    def obs_copy(d):
        return remote(
            obs_in.at[chip], obs_in.at[chip], o_send.at[d], o_recv.at[d], chip_peer(d)[1]
        )

    each(chips, lambda d: obs_copy(d).start())
    keep.wait()

    def products_of(start, size):
        block = gathered[:, :, start:start + size].reshape(members, size)
        return lax.dot_general(block, block, (((1,), (1,)), ((), ())), preferred_element_type=F32)

    start = 0
    for index, eighths in enumerate(SPREAD):
        each(groups, lambda d: spread(index, start, d).wait_recv())
        if start:
            products[...] += products_of(start * unit, eighths * unit)
        else:
            products[...] = products_of(0, eighths * unit)
        start += eighths
    cross = products[...]
    row_index = lax.broadcasted_iota(jnp.int32, (members, members), 0)
    col_index = lax.broadcasted_iota(jnp.int32, (members, members), 1)
    diagonal = jnp.where(row_index == col_index, cross, 0.0)
    norm_rows = jnp.sum(diagonal, axis=1, keepdims=True)
    norm_cols = jnp.sum(diagonal, axis=0, keepdims=True)
    pair_sq = norm_rows + norm_cols - 2.0 * cross
    half = members // 2
    small_row = lax.broadcasted_iota(jnp.int32, (half, half), 0)
    small_col = lax.broadcasted_iota(jnp.int32, (half, half), 1)
    upper = small_col > small_row
    lower = small_col < small_row
    share = members // teams
    part[: teams // 2] = pair_sq[:half, half:].reshape(teams // 2, share, half)
    part[teams // 2 :] = jnp.where(upper, pair_sq[:half, :half], pair_sq[half:, half:]).reshape(
        teams // 2, share, half
    )

    def part_copy(d):
        other, device = team_peer(d)
        return remote(part.at[other], part_in.at[rank], p_send.at[d], p_recv.at[d], device)

    def chip_copy(d):
        return remote(
            chip_in.at[chip], chip_in.at[chip], c_send.at[d], c_recv.at[d], chip_peer(d)[1]
        )

    def sum_copy(d):
        return remote(
            summed.at[rank], summed.at[rank], s_send.at[d], s_recv.at[d], team_peer(d)[1]
        )

    each(teams, lambda d: part_copy(d).start())
    part_in[rank] = part[rank]
    each(teams, lambda d: part_copy(d).wait_recv())
    chip_in[chip] = jnp.sum(part_in[...], axis=0)
    each(chips, lambda d: chip_copy(d).start())
    each(chips, lambda d: chip_copy(d).wait_recv())
    summed[rank] = jnp.sum(chip_in[...], axis=0)
    each(teams, lambda d: sum_copy(d).start())
    each(teams, lambda d: sum_copy(d).wait_recv())

    off = 1.0 / jnp.sqrt(summed[: teams // 2].reshape(half, half))
    triangles = summed[teams // 2 :].reshape(half, half)
    triangles = jnp.where(small_row == small_col, 1.0, triangles)
    triangles = 1.0 / jnp.sqrt(triangles)
    above = jnp.where(upper, triangles, 0.0)
    below = jnp.where(lower, triangles, 0.0)
    first = above + above.T
    second = below + below.T
    off_t = off.T
    def slope_of(own_part, own_products, cross_part, cross_products):
        along = jnp.sum(own_part * own_products + cross_part * cross_products, axis=1, keepdims=True)
        square = jnp.sum(jnp.where(small_row == small_col, own_products, 0.0), axis=1, keepdims=True)
        slope = jnp.where(square > 0.0, along / jnp.where(square > 0.0, square, 1.0), 0.0)
        return slope.astype(BF16).astype(F32)

    slope_first = slope_of(first, products[:half, :half], off, products[:half, half:])
    slope_second = slope_of(second, products[half:, half:], off_t, products[half:, :half])
    low[:half, :half] = jnp.where(small_row == small_col, -slope_first, first).astype(BF16)
    low[:half, half:] = off.astype(BF16)
    low[half:, :half] = off_t.astype(BF16)
    low[half:, half:] = jnp.where(small_row == small_col, -slope_second, second).astype(BF16)
    slopes = jnp.concatenate([slope_first, slope_second], axis=0)
    slopes = jnp.broadcast_to(slopes, (members, 128)).reshape(groups, rows, 128)
    lines[...] = slopes
    total_first = jnp.sum(first + off, axis=1, keepdims=True)
    total_second = jnp.sum(second + off_t, axis=1, keepdims=True)
    groups_half = groups // 2
    totals[:groups_half] = jnp.broadcast_to(total_first, (half, 128)).reshape(groups_half, rows, 128)
    totals[groups_half:] = jnp.broadcast_to(total_second, (half, 128)).reshape(
        groups_half, rows, 128
    )

    def weigh(i, top):
        at = chunk_at(i)
        block = gathered[:, :, at].reshape(members, CHUNK)
        rest = jnp.dot(low[...], block, preferred_element_type=F32)
        weighted[:, :, at] = rest.reshape(groups, rows, CHUNK)
        rest = jnp.abs(rest)
        for k in range(CHUNK // 128):
            top = jnp.maximum(top, rest[:, k * 128:(k + 1) * 128])
        return top

    share_rows = rows // 2
    lane = lax.broadcasted_iota(jnp.int32, (groups, share_rows, TILE), 2)

    def give(message, base, size, d):
        other, device = group_peer(d)
        at = message * groups + d
        span = pl.ds(base, size)
        return remote(
            sent.at[other, :, span], got.at[me, :, span], r_send.at[at], r_recv.at[at], device
        )

    sizes = []
    start, base, message = 0, 0, 0
    for parts in RETURN:
        first_step, last_step = start * steps, (start + sum(parts)) * steps
        top = lax.fori_loop(first_step, last_step, weigh, jnp.zeros((members, 128), F32))
        top = jnp.max(top, axis=1, keepdims=True)
        scale = jnp.maximum(top * 1.0079, 1e-30).astype(BF16).astype(F32)
        scale = jnp.broadcast_to(scale, (members, 128)).reshape(groups, rows, 128)
        inverses[...] = RANGE / scale
        heads = jnp.where(lane < 32, scale[:, :share_rows], slopes[:, :share_rows])
        tails = jnp.where(lane < 96, scale[:, share_rows:], slopes[:, share_rows:])
        sent[:, :, base:base + TILE] = jnp.where(lane < 64, heads, tails).astype(BF16)
        first_size = TILE + 2 * parts[0] * unit

        def encode(d):
            other = group_peer(d)[0]
            inverse = inverses[other]
            place_at, step_at = base + TILE, first_step
            for eighths in parts:
                width = eighths * unit

                def code(i, _, place_at=place_at, step_at=step_at, width=width):
                    rest = weighted[other, :, chunk_at(i + step_at)]
                    coded = jnp.exp2(rest * wide(inverse)).astype(BF16)
                    early = pl.ds(pl.multiple_of(place_at + i * CHUNK, 128), CHUNK)
                    late = pl.ds(pl.multiple_of(place_at + width + i * CHUNK, 128), CHUNK)
                    sent[other, :, early] = coded[:share_rows]
                    sent[other, :, late] = coded[share_rows:]
                    return 0

                lax.fori_loop(0, eighths * steps, code, 0)
                place_at, step_at = place_at + 2 * width, step_at + eighths * steps
            give(message, base, first_size, d).start()

        each(groups, encode)
        sizes.append((base, first_size))
        base += first_size
        message += 1
        for eighths in parts[1:]:
            size = 2 * eighths * unit
            each(groups, lambda d: give(message, base, size, d).start())
            sizes.append((base, size))
            base += size
            message += 1
        start += sum(parts)

    each(chips, lambda d: obs_copy(d).wait_recv())
    obs = jnp.sqrt(jnp.sum(jnp.sum(obs_in[:chips], axis=0), axis=1, keepdims=True))
    near = jnp.broadcast_to(factor / obs, (rows, 128))
    share_factor = factor / members
    row_total = totals[me]

    def fill(piece, offset, count, along_own, value_at):
        def one(i, _):
            point = pl.ds(pl.multiple_of(piece * cols + offset + i * CHUNK, CHUNK), CHUNK)
            ours = own[:, point].astype(F32) * wide(along_own)
            out[:, point] = ours - analysis[:, point] * wide(near) + value_at(i)
            return 0

        lax.fori_loop(0, count, one, 0)

    fill(
        me, 0, cols // CHUNK, near - (row_total - lines[me]) * share_factor,
        lambda i: weighted[me, :, chunk_at(i)] * share_factor,
    )
    start, base, message = 0, 0, 0
    for parts in RETURN:
        tile_at = base
        base += TILE
        for nth, eighths in enumerate(parts):
            width = eighths * unit

            def take(d):
                give(message, *sizes[message], d).wait_recv()
                piece = group_source(d)

                def decode(i, scale):
                    early = pl.ds(pl.multiple_of(base + i * CHUNK, 128), CHUNK)
                    late = pl.ds(pl.multiple_of(base + width + i * CHUNK, 128), CHUNK)
                    coded = jnp.concatenate([got[piece, :, early], got[piece, :, late]], axis=0)
                    return jnp.log(coded.astype(F32)) * wide(scale)

                def add(i, _):
                    point = piece * cols + start * unit + i * CHUNK
                    point = pl.ds(pl.multiple_of(point, CHUNK), CHUNK)
                    out[:, point] += decode(i, inverses[piece])
                    return 0

                if nth:
                    lax.fori_loop(0, eighths * steps, add, 0)
                    return
                tile = got[piece, :, tile_at:tile_at + TILE].astype(F32)
                scale = jnp.concatenate([tile[:, :1], tile[:, 64:65]], axis=0)
                scale = jnp.broadcast_to(scale * (share_factor / (RANGE * LN2)), (rows, 128))
                inverses[piece] = scale
                slope = jnp.concatenate([tile[:, 32:33], tile[:, 96:97]], axis=0)
                along_own = near - (row_total - jnp.broadcast_to(slope, (rows, 128))) * share_factor
                fill(piece, start * unit, eighths * steps, along_own, lambda i: decode(i, scale))
                fill(
                    piece, (start + eighths) * unit, sum(parts[1:]) * steps, along_own,
                    lambda i: 0.0,
                )

            each(groups, take)
            base += 2 * width
            start += eighths
            message += 1

    start = 0
    for index, eighths in enumerate(SPREAD):
        each(groups, lambda d: spread(index, start, d).wait_send())
        start += eighths
    each(chips, lambda d: obs_copy(d).wait_send())
    each(teams, lambda d: part_copy(d).wait_send())
    each(chips, lambda d: chip_copy(d).wait_send())
    each(teams, lambda d: sum_copy(d).wait_send())
    for message, (base, size) in enumerate(sizes):
        each(groups, lambda d: give(message, base, size, d).wait_send())


def on_device(ensemble, analysis):
    rows, points = ensemble.shape
    groups = lax.axis_size("member")
    places = lax.axis_size("space")
    chips = places // 2
    teams = groups * 2
    members = rows * groups
    cols = points // groups
    half = members // 2
    share = members // teams
    factor = math.sqrt(points * places)
    messages = sum(len(parts) for parts in RETURN)
    dma = pltpu.SemaphoreType.DMA
    return pl.pallas_call(
        functools.partial(kernel, groups, chips, factor),
        out_shape=pltpu.VMEM((rows, points), F32),
        in_specs=[pl.BlockSpec(memory_space=pltpu.HBM)] * 2,
        out_specs=pl.BlockSpec(memory_space=pltpu.VMEM),
        scratch_shapes=[
            pltpu.VMEM((groups, rows, cols), BF16),
            pltpu.VMEM((rows, points), BF16),
            pltpu.VMEM((1, points), F32),
            pltpu.VMEM((groups, rows, cols), F32),
            pltpu.VMEM((groups, rows // 2, 2 * cols + len(RETURN) * TILE), BF16),
            pltpu.VMEM((groups, rows // 2, 2 * cols + len(RETURN) * TILE), BF16),
            pltpu.VMEM((members, members), F32),
            pltpu.VMEM((teams, share, half), F32),
            pltpu.VMEM((teams, share, half), F32),
            pltpu.VMEM((chips, share, half), F32),
            pltpu.VMEM((teams, share, half), F32),
            pltpu.VMEM((members, members), BF16),
            pltpu.VMEM((groups, rows, 128), F32),
            pltpu.VMEM((groups, rows, 128), F32),
            pltpu.VMEM((groups, rows, 128), F32),
            pltpu.VMEM((chips + 2, rows, 128), F32),
            dma((len(SPREAD) * groups,)), dma((len(SPREAD) * groups,)),
            dma((teams,)), dma((teams,)),
            dma((chips,)), dma((chips,)),
            dma((teams,)), dma((teams,)),
            dma((messages * groups,)), dma((messages * groups,)),
            dma((chips,)), dma((chips,)),
            dma((3,)),
        ],
        compiler_params=pltpu.CompilerParams(
            collective_id=0, has_side_effects=True, vmem_limit_bytes=56 * 2**20
        ),
        cost_estimate=pl.CostEstimate(
            flops=4 * members * members * cols, bytes_accessed=8 * rows * points, transcendentals=0
        ),
    )(ensemble, analysis.reshape(1, points))


def solution(mesh):
    placed = (P("member", "space"), P("space"))
    return jax.shard_map(
        on_device, mesh=mesh, in_specs=placed, out_specs=P("member", "space"), check_vma=False
    )
```

```python
import functools
import math

import jax
import jax.numpy as jnp
from jax import lax
from jax.experimental import pallas as pl
from jax.experimental.pallas import tpu as pltpu
from jax.sharding import PartitionSpec as P

MESH = pl.DeviceIdType.MESH
F32 = jnp.float32
BF16 = jnp.bfloat16
RANGE = 125.0
LN2 = math.log(2.0)
CHUNK = 512
SPREAD = (3, 3, 2)
RETURN = ((1,), (5, 2))
TILE = 128
CHIP_STEPS = ((2, 1), (1, 1), (3, 1), (2, 0), (0, 1), (1, 0), (3, 0))
STEPS = ((2, 1), (2, 0), (3, 1), (1, 1), (0, 1), (3, 0), (1, 0))


def chunk_at(index):
    return pl.ds(pl.multiple_of(index * CHUNK, CHUNK), CHUNK)


def wide(tile):
    return jnp.concatenate([tile] * (CHUNK // 128), axis=1)


def kernel(
    groups, chips, factor, x_hbm, a_hbm, out,
    gathered, own, analysis, weighted, sent, got,
    products, part, part_in, chip_in, summed, low, totals, lines, inverses, obs_in,
    x_send, x_recv, p_send, p_recv, c_send, c_recv, s_send, s_recv, r_send, r_recv,
    o_send, o_recv, local_sem,
):
    me = lax.axis_index("member")
    place = lax.axis_index("space")
    core = lax.rem(place, 2)
    chip = place // 2
    rank = me * 2 + core
    teams = groups * 2
    rows = own.shape[0]
    cols = gathered.shape[2]
    members = groups * rows
    unit = cols // 8
    steps = unit // CHUNK

    def each(count, body):
        for d in range(1, count):
            body(d)

    def columns(index):
        return pl.ds(pl.multiple_of(index * cols, cols), cols)

    def group_peer(d):
        dz, dy = STEPS[d - 1]
        other = lax.rem(me // 2 + dz, groups // 2) * 2 + lax.rem(me + dy, 2)
        return other, (other, place)

    def group_source(d):
        dz, dy = STEPS[d - 1]
        return lax.rem(me // 2 + groups // 2 - dz, groups // 2) * 2 + lax.rem(me + dy, 2)

    def team_peer(d):
        member = group_peer((d + 1) // 2)[0] if d < teams - 1 else me
        its_core = core if d % 2 == 0 else 1 - core
        return member * 2 + its_core, (member, chip * 2 + its_core)

    def chip_peer(d):
        dx, dy = CHIP_STEPS[d - 1]
        other = lax.rem(chip // 2 + dx, chips // 2) * 2 + lax.rem(chip + dy, 2)
        return other, (me, other * 2 + core)

    sibling = (me, chip * 2 + 1 - core)

    def remote(src, dst, send, recv, device):
        return pltpu.make_async_remote_copy(
            src_ref=src, dst_ref=dst, send_sem=send, recv_sem=recv,
            device_id=device, device_id_type=MESH,
        )

    barrier = pltpu.get_barrier_semaphore()

    def greet(device):
        pl.semaphore_signal(barrier, inc=1, device_id=device, device_id_type=MESH)

    greet(sibling)
    each(groups, lambda d: greet(group_peer(d)[1]))
    each(chips, lambda d: greet(chip_peer(d)[1]))

    load_analysis = pltpu.make_async_copy(a_hbm, analysis, local_sem.at[0])
    load_analysis.start()
    load_own = pltpu.make_async_copy(x_hbm, own, local_sem.at[1])
    load_own.start()
    keep = pltpu.make_async_copy(x_hbm.at[:, columns(me)], gathered.at[me], local_sem.at[2])
    keep.start()

    pl.semaphore_wait(barrier, groups + chips - 1)

    def spread(index, start, d):
        width = SPREAD[index] * unit
        other, device = group_peer(d)
        src = pl.ds(pl.multiple_of(other * cols + start * unit, unit), width)
        at = index * groups + d
        return remote(
            x_hbm.at[:, src], gathered.at[me, :, pl.ds(start * unit, width)],
            x_send.at[at], x_recv.at[at], device,
        )

    start = 0
    for index, eighths in enumerate(SPREAD):
        each(groups, lambda d: spread(index, start, d).start())
        start += eighths

    load_analysis.wait()
    load_own.wait()

    def add_distance(i, total):
        at = chunk_at(i)
        deviation = own[:, at].astype(F32) - analysis[:, at]
        square = deviation * deviation
        for k in range(CHUNK // 128):
            total = total + square[:, k * 128:(k + 1) * 128]
        return total

    distance = lax.fori_loop(0, own.shape[1] // CHUNK, add_distance, jnp.zeros((rows, 128), F32))
    obs_in[chips] = distance
    pair = remote(obs_in.at[chips], obs_in.at[chips + 1], o_send.at[0], o_recv.at[0], sibling)
    pair.start()
    pair.wait()
    obs_in[chip] = distance + obs_in[chips + 1]

    def obs_copy(d):
        return remote(
            obs_in.at[chip], obs_in.at[chip], o_send.at[d], o_recv.at[d], chip_peer(d)[1]
        )

    each(chips, lambda d: obs_copy(d).start())
    keep.wait()

    def products_of(start, size):
        block = gathered[:, :, start:start + size].reshape(members, size)
        return lax.dot_general(block, block, (((1,), (1,)), ((), ())), preferred_element_type=F32)

    start = 0
    for index, eighths in enumerate(SPREAD):
        each(groups, lambda d: spread(index, start, d).wait_recv())
        if start:
            products[...] += products_of(start * unit, eighths * unit)
        else:
            products[...] = products_of(0, eighths * unit)
        start += eighths
    cross = products[...]
    row_index = lax.broadcasted_iota(jnp.int32, (members, members), 0)
    col_index = lax.broadcasted_iota(jnp.int32, (members, members), 1)
    diagonal = jnp.where(row_index == col_index, cross, 0.0)
    norm_rows = jnp.sum(diagonal, axis=1, keepdims=True)
    norm_cols = jnp.sum(diagonal, axis=0, keepdims=True)
    pair_sq = norm_rows + norm_cols - 2.0 * cross
    half = members // 2
    small_row = lax.broadcasted_iota(jnp.int32, (half, half), 0)
    small_col = lax.broadcasted_iota(jnp.int32, (half, half), 1)
    upper = small_col > small_row
    lower = small_col < small_row
    share = members // teams
    part[: teams // 2] = pair_sq[:half, half:].reshape(teams // 2, share, half)
    part[teams // 2 :] = jnp.where(upper, pair_sq[:half, :half], pair_sq[half:, half:]).reshape(
        teams // 2, share, half
    )

    def part_copy(d):
        other, device = team_peer(d)
        return remote(part.at[other], part_in.at[rank], p_send.at[d], p_recv.at[d], device)

    def chip_copy(d):
        return remote(
            chip_in.at[chip], chip_in.at[chip], c_send.at[d], c_recv.at[d], chip_peer(d)[1]
        )

    def sum_copy(d):
        return remote(
            summed.at[rank], summed.at[rank], s_send.at[d], s_recv.at[d], team_peer(d)[1]
        )

    each(teams, lambda d: part_copy(d).start())
    part_in[rank] = part[rank]
    each(teams, lambda d: part_copy(d).wait_recv())
    chip_in[chip] = jnp.sum(part_in[...], axis=0)
    each(chips, lambda d: chip_copy(d).start())
    each(chips, lambda d: chip_copy(d).wait_recv())
    summed[rank] = jnp.sum(chip_in[...], axis=0)
    each(teams, lambda d: sum_copy(d).start())
    each(teams, lambda d: sum_copy(d).wait_recv())

    off = 1.0 / jnp.sqrt(summed[: teams // 2].reshape(half, half))
    triangles = summed[teams // 2 :].reshape(half, half)
    triangles = jnp.where(small_row == small_col, 1.0, triangles)
    triangles = 1.0 / jnp.sqrt(triangles)
    above = jnp.where(upper, triangles, 0.0)
    below = jnp.where(lower, triangles, 0.0)
    first = above + above.T
    second = below + below.T
    off_t = off.T
    def slope_of(own_part, own_products, cross_part, cross_products, square):
        along = jnp.sum(own_part * own_products + cross_part * cross_products, axis=1, keepdims=True)
        slope = jnp.where(square > 0.0, along / jnp.where(square > 0.0, square, 1.0), 0.0)
        return slope.astype(BF16).astype(F32)

    slope_first = slope_of(first, products[:half, :half], off, products[:half, half:], norm_rows[:half])
    slope_second = slope_of(second, products[half:, half:], off_t, products[half:, :half], norm_rows[half:])
    low[:half, :half] = jnp.where(small_row == small_col, -slope_first, first).astype(BF16)
    low[:half, half:] = off.astype(BF16)
    low[half:, :half] = off_t.astype(BF16)
    low[half:, half:] = jnp.where(small_row == small_col, -slope_second, second).astype(BF16)
    slopes = jnp.concatenate([slope_first, slope_second], axis=0)
    slopes = jnp.broadcast_to(slopes, (members, 128)).reshape(groups, rows, 128)
    lines[...] = slopes
    total_first = jnp.sum(first + off, axis=1, keepdims=True)
    total_second = jnp.sum(second + off_t, axis=1, keepdims=True)
    groups_half = groups // 2
    totals[:groups_half] = jnp.broadcast_to(total_first, (half, 128)).reshape(groups_half, rows, 128)
    totals[groups_half:] = jnp.broadcast_to(total_second, (half, 128)).reshape(
        groups_half, rows, 128
    )

    def weigh(i, top):
        at = chunk_at(i)
        block = gathered[:, :, at].reshape(members, CHUNK)
        rest = jnp.dot(low[...], block, preferred_element_type=F32)
        weighted[:, :, at] = rest.reshape(groups, rows, CHUNK)
        rest = jnp.abs(rest)
        for k in range(CHUNK // 128):
            top = jnp.maximum(top, rest[:, k * 128:(k + 1) * 128])
        return top

    share_rows = rows // 2
    lane = lax.broadcasted_iota(jnp.int32, (groups, share_rows, TILE), 2)

    def give(message, base, size, d):
        other, device = group_peer(d)
        at = message * groups + d
        span = pl.ds(base, size)
        return remote(
            sent.at[other, :, span], got.at[me, :, span], r_send.at[at], r_recv.at[at], device
        )

    sizes = []
    start, base, message = 0, 0, 0
    for parts in RETURN:
        first_step, last_step = start * steps, (start + sum(parts)) * steps
        top = lax.fori_loop(first_step, last_step, weigh, jnp.zeros((members, 128), F32))
        top = jnp.max(top, axis=1, keepdims=True)
        scale = jnp.maximum(top * 1.0079, 1e-30).astype(BF16).astype(F32)
        scale = jnp.broadcast_to(scale, (members, 128)).reshape(groups, rows, 128)
        inverses[...] = RANGE / scale
        heads = jnp.where(lane < 32, scale[:, :share_rows], slopes[:, :share_rows])
        tails = jnp.where(lane < 96, scale[:, share_rows:], slopes[:, share_rows:])
        sent[:, :, base:base + TILE] = jnp.where(lane < 64, heads, tails).astype(BF16)
        first_size = TILE + 2 * parts[0] * unit

        def encode(d):
            other = group_peer(d)[0]
            inverse = inverses[other]
            place_at, step_at = base + TILE, first_step
            for eighths in parts:
                width = eighths * unit

                def code(i, _, place_at=place_at, step_at=step_at, width=width):
                    rest = weighted[other, :, chunk_at(i + step_at)]
                    coded = jnp.exp2(rest * wide(inverse)).astype(BF16)
                    early = pl.ds(pl.multiple_of(place_at + i * CHUNK, 128), CHUNK)
                    late = pl.ds(pl.multiple_of(place_at + width + i * CHUNK, 128), CHUNK)
                    sent[other, :, early] = coded[:share_rows]
                    sent[other, :, late] = coded[share_rows:]
                    return 0

                lax.fori_loop(0, eighths * steps, code, 0)
                place_at, step_at = place_at + 2 * width, step_at + eighths * steps
            give(message, base, first_size, d).start()

        each(groups, encode)
        sizes.append((base, first_size))
        base += first_size
        message += 1
        for eighths in parts[1:]:
            size = 2 * eighths * unit
            each(groups, lambda d: give(message, base, size, d).start())
            sizes.append((base, size))
            base += size
            message += 1
        start += sum(parts)

    each(chips, lambda d: obs_copy(d).wait_recv())
    obs = jnp.sqrt(jnp.sum(jnp.sum(obs_in[:chips], axis=0), axis=1, keepdims=True))
    near = jnp.broadcast_to(factor / obs, (rows, 128))
    share_factor = factor / members
    row_total = totals[me]

    def fill(piece, offset, count, along_own, value_at):
        def one(i, _):
            point = pl.ds(pl.multiple_of(piece * cols + offset + i * CHUNK, CHUNK), CHUNK)
            ours = own[:, point].astype(F32) * wide(along_own)
            out[:, point] = ours - analysis[:, point] * wide(near) + value_at(i)
            return 0

        lax.fori_loop(0, count, one, 0)

    fill(
        me, 0, cols // CHUNK, near - (row_total - lines[me]) * share_factor,
        lambda i: weighted[me, :, chunk_at(i)] * share_factor,
    )
    start = 0
    for index, eighths in enumerate(SPREAD):
        each(groups, lambda d: spread(index, start, d).wait_send())
        start += eighths
    each(chips, lambda d: obs_copy(d).wait_send())
    each(teams, lambda d: part_copy(d).wait_send())
    each(chips, lambda d: chip_copy(d).wait_send())
    each(teams, lambda d: sum_copy(d).wait_send())
    start, base, message = 0, 0, 0
    for parts in RETURN:
        tile_at = base
        base += TILE
        for nth, eighths in enumerate(parts):
            width = eighths * unit

            def take(d):
                give(message, *sizes[message], d).wait_recv()
                piece = group_source(d)

                def decode(i, scale):
                    early = pl.ds(pl.multiple_of(base + i * CHUNK, 128), CHUNK)
                    late = pl.ds(pl.multiple_of(base + width + i * CHUNK, 128), CHUNK)
                    coded = jnp.concatenate([got[piece, :, early], got[piece, :, late]], axis=0)
                    return jnp.log(coded.astype(F32)) * wide(scale)

                def add(i, _):
                    point = piece * cols + start * unit + i * CHUNK
                    point = pl.ds(pl.multiple_of(point, CHUNK), CHUNK)
                    out[:, point] += decode(i, inverses[piece])
                    return 0

                if nth:
                    lax.fori_loop(0, eighths * steps, add, 0)
                    return
                tile = got[piece, :, tile_at:tile_at + TILE].astype(F32)
                scale = jnp.concatenate([tile[:, :1], tile[:, 64:65]], axis=0)
                scale = jnp.broadcast_to(scale * (share_factor / (RANGE * LN2)), (rows, 128))
                inverses[piece] = scale
                slope = jnp.concatenate([tile[:, 32:33], tile[:, 96:97]], axis=0)
                along_own = near - (row_total - jnp.broadcast_to(slope, (rows, 128))) * share_factor
                fill(piece, start * unit, eighths * steps, along_own, lambda i: decode(i, scale))
                fill(
                    piece, (start + eighths) * unit, sum(parts[1:]) * steps, along_own,
                    lambda i: 0.0,
                )

            each(groups, take)
            if message:
                each(groups, lambda d: give(message - 1, *sizes[message - 1], d).wait_send())
            base += 2 * width
            start += eighths
            message += 1

    each(groups, lambda d: give(message - 1, *sizes[message - 1], d).wait_send())


def on_device(ensemble, analysis):
    rows, points = ensemble.shape
    groups = lax.axis_size("member")
    places = lax.axis_size("space")
    chips = places // 2
    teams = groups * 2
    members = rows * groups
    cols = points // groups
    half = members // 2
    share = members // teams
    factor = math.sqrt(points * places)
    messages = sum(len(parts) for parts in RETURN)
    dma = pltpu.SemaphoreType.DMA
    return pl.pallas_call(
        functools.partial(kernel, groups, chips, factor),
        out_shape=pltpu.VMEM((rows, points), F32),
        in_specs=[pl.BlockSpec(memory_space=pltpu.HBM)] * 2,
        out_specs=pl.BlockSpec(memory_space=pltpu.VMEM),
        scratch_shapes=[
            pltpu.VMEM((groups, rows, cols), BF16),
            pltpu.VMEM((rows, points), BF16),
            pltpu.VMEM((1, points), F32),
            pltpu.VMEM((groups, rows, cols), F32),
            pltpu.VMEM((groups, rows // 2, 2 * cols + len(RETURN) * TILE), BF16),
            pltpu.VMEM((groups, rows // 2, 2 * cols + len(RETURN) * TILE), BF16),
            pltpu.VMEM((members, members), F32),
            pltpu.VMEM((teams, share, half), F32),
            pltpu.VMEM((teams, share, half), F32),
            pltpu.VMEM((chips, share, half), F32),
            pltpu.VMEM((teams, share, half), F32),
            pltpu.VMEM((members, members), BF16),
            pltpu.VMEM((groups, rows, 128), F32),
            pltpu.VMEM((groups, rows, 128), F32),
            pltpu.VMEM((groups, rows, 128), F32),
            pltpu.VMEM((chips + 2, rows, 128), F32),
            dma((len(SPREAD) * groups,)), dma((len(SPREAD) * groups,)),
            dma((teams,)), dma((teams,)),
            dma((chips,)), dma((chips,)),
            dma((teams,)), dma((teams,)),
            dma((messages * groups,)), dma((messages * groups,)),
            dma((chips,)), dma((chips,)),
            dma((3,)),
        ],
        compiler_params=pltpu.CompilerParams(
            collective_id=0, has_side_effects=True, vmem_limit_bytes=56 * 2**20
        ),
        cost_estimate=pl.CostEstimate(
            flops=4 * members * members * cols, bytes_accessed=8 * rows * points, transcendentals=0
        ),
    )(ensemble, analysis.reshape(1, points))


def solution(mesh):
    placed = (P("member", "space"), P("space"))
    return jax.shard_map(
        on_device, mesh=mesh, in_specs=placed, out_specs=P("member", "space"), check_vma=False
    )
```

```python
import functools
import math

import jax
import jax.numpy as jnp
from jax import lax
from jax.experimental import pallas as pl
from jax.experimental.pallas import tpu as pltpu
from jax.sharding import PartitionSpec as P

MESH = pl.DeviceIdType.MESH
F32 = jnp.float32
BF16 = jnp.bfloat16
RANGE = 125.0
LN2 = math.log(2.0)
CHUNK = 512
SPREAD = (3, 3, 2)
RETURN = ((1,), (6, 1))
TILE = 128
CHIP_STEPS = ((2, 1), (1, 1), (3, 1), (2, 0), (0, 1), (1, 0), (3, 0))
STEPS = ((2, 1), (2, 0), (3, 1), (1, 1), (0, 1), (3, 0), (1, 0))


def chunk_at(index):
    return pl.ds(pl.multiple_of(index * CHUNK, CHUNK), CHUNK)


def wide(tile):
    return jnp.concatenate([tile] * (CHUNK // 128), axis=1)


def kernel(
    groups, chips, factor, x_hbm, a_hbm, out,
    gathered, own, analysis, weighted, sent, got,
    products, part, part_in, chip_in, summed, low, totals, lines, inverses, obs_in,
    x_send, x_recv, p_send, p_recv, c_send, c_recv, s_send, s_recv, r_send, r_recv,
    o_send, o_recv, local_sem,
):
    me = lax.axis_index("member")
    place = lax.axis_index("space")
    core = lax.rem(place, 2)
    chip = place // 2
    rank = me * 2 + core
    teams = groups * 2
    rows = own.shape[0]
    cols = gathered.shape[2]
    members = groups * rows
    unit = cols // 8
    steps = unit // CHUNK

    def each(count, body):
        for d in range(1, count):
            body(d)

    def columns(index):
        return pl.ds(pl.multiple_of(index * cols, cols), cols)

    def group_peer(d):
        dz, dy = STEPS[d - 1]
        other = lax.rem(me // 2 + dz, groups // 2) * 2 + lax.rem(me + dy, 2)
        return other, (other, place)

    def group_source(d):
        dz, dy = STEPS[d - 1]
        return lax.rem(me // 2 + groups // 2 - dz, groups // 2) * 2 + lax.rem(me + dy, 2)

    def team_peer(d):
        nth = (d - 1) % (groups - 1) + 1
        member = group_peer(nth)[0] if d < teams - 1 else me
        its_core = core if d < groups else 1 - core
        return member * 2 + its_core, (member, chip * 2 + its_core)

    def chip_peer(d):
        dx, dy = CHIP_STEPS[d - 1]
        other = lax.rem(chip // 2 + dx, chips // 2) * 2 + lax.rem(chip + dy, 2)
        return other, (me, other * 2 + core)

    sibling = (me, chip * 2 + 1 - core)

    def remote(src, dst, send, recv, device):
        return pltpu.make_async_remote_copy(
            src_ref=src, dst_ref=dst, send_sem=send, recv_sem=recv,
            device_id=device, device_id_type=MESH,
        )

    barrier = pltpu.get_barrier_semaphore()

    def greet(device):
        pl.semaphore_signal(barrier, inc=1, device_id=device, device_id_type=MESH)

    greet(sibling)
    each(groups, lambda d: greet(group_peer(d)[1]))
    each(chips, lambda d: greet(chip_peer(d)[1]))

    load_analysis = pltpu.make_async_copy(a_hbm, analysis, local_sem.at[0])
    load_analysis.start()
    load_own = pltpu.make_async_copy(x_hbm, own, local_sem.at[1])
    load_own.start()
    keep = pltpu.make_async_copy(x_hbm.at[:, columns(me)], gathered.at[me], local_sem.at[2])
    keep.start()

    pl.semaphore_wait(barrier, groups + chips - 1)

    def spread(index, start, d):
        width = SPREAD[index] * unit
        other, device = group_peer(d)
        src = pl.ds(pl.multiple_of(other * cols + start * unit, unit), width)
        at = index * groups + d
        return remote(
            x_hbm.at[:, src], gathered.at[me, :, pl.ds(start * unit, width)],
            x_send.at[at], x_recv.at[at], device,
        )

    start = 0
    for index, eighths in enumerate(SPREAD):
        each(groups, lambda d: spread(index, start, d).start())
        start += eighths

    load_analysis.wait()
    load_own.wait()

    def add_distance(i, total):
        at = chunk_at(i)
        deviation = own[:, at].astype(F32) - analysis[:, at]
        square = deviation * deviation
        for k in range(CHUNK // 128):
            total = total + square[:, k * 128:(k + 1) * 128]
        return total

    distance = lax.fori_loop(0, own.shape[1] // CHUNK, add_distance, jnp.zeros((rows, 128), F32))
    obs_in[chips] = distance
    pair = remote(obs_in.at[chips], obs_in.at[chips + 1], o_send.at[0], o_recv.at[0], sibling)
    pair.start()
    pair.wait()
    obs_in[chip] = distance + obs_in[chips + 1]

    def obs_copy(d):
        return remote(
            obs_in.at[chip], obs_in.at[chip], o_send.at[d], o_recv.at[d], chip_peer(d)[1]
        )

    each(chips, lambda d: obs_copy(d).start())
    keep.wait()

    def products_of(start, size):
        block = gathered[:, :, start:start + size].reshape(members, size)
        return lax.dot_general(block, block, (((1,), (1,)), ((), ())), preferred_element_type=F32)

    start = 0
    for index, eighths in enumerate(SPREAD):
        each(groups, lambda d: spread(index, start, d).wait_recv())
        if start:
            products[...] += products_of(start * unit, eighths * unit)
        else:
            products[...] = products_of(0, eighths * unit)
        start += eighths
    cross = products[...]
    row_index = lax.broadcasted_iota(jnp.int32, (members, members), 0)
    col_index = lax.broadcasted_iota(jnp.int32, (members, members), 1)
    diagonal = jnp.where(row_index == col_index, cross, 0.0)
    norm_rows = jnp.sum(diagonal, axis=1, keepdims=True)
    norm_cols = jnp.sum(diagonal, axis=0, keepdims=True)
    pair_sq = norm_rows + norm_cols - 2.0 * cross
    half = members // 2
    small_row = lax.broadcasted_iota(jnp.int32, (half, half), 0)
    small_col = lax.broadcasted_iota(jnp.int32, (half, half), 1)
    upper = small_col > small_row
    lower = small_col < small_row
    share = members // teams
    part[: teams // 2] = pair_sq[:half, half:].reshape(teams // 2, share, half)
    part[teams // 2 :] = jnp.where(upper, pair_sq[:half, :half], pair_sq[half:, half:]).reshape(
        teams // 2, share, half
    )

    def part_copy(d):
        other, device = team_peer(d)
        return remote(part.at[other], part_in.at[rank], p_send.at[d], p_recv.at[d], device)

    def chip_copy(d):
        return remote(
            chip_in.at[chip], chip_in.at[chip], c_send.at[d], c_recv.at[d], chip_peer(d)[1]
        )

    def sum_copy(d):
        return remote(
            summed.at[rank], summed.at[rank], s_send.at[d], s_recv.at[d], team_peer(d)[1]
        )

    each(teams, lambda d: part_copy(d).start())
    part_in[rank] = part[rank]
    each(teams, lambda d: part_copy(d).wait_recv())
    chip_in[chip] = jnp.sum(part_in[...], axis=0)
    each(chips, lambda d: chip_copy(d).start())
    each(chips, lambda d: chip_copy(d).wait_recv())
    summed[rank] = jnp.sum(chip_in[...], axis=0)
    each(teams, lambda d: sum_copy(d).start())
    each(teams, lambda d: sum_copy(d).wait_recv())

    off = 1.0 / jnp.sqrt(summed[: teams // 2].reshape(half, half))
    triangles = summed[teams // 2 :].reshape(half, half)
    triangles = jnp.where(small_row == small_col, 1.0, triangles)
    triangles = 1.0 / jnp.sqrt(triangles)
    above = jnp.where(upper, triangles, 0.0)
    below = jnp.where(lower, triangles, 0.0)
    first = above + above.T
    second = below + below.T
    off_t = off.T
    def slope_of(own_part, own_products, cross_part, cross_products, square):
        along = jnp.sum(own_part * own_products + cross_part * cross_products, axis=1, keepdims=True)
        slope = jnp.where(square > 0.0, along / jnp.where(square > 0.0, square, 1.0), 0.0)
        return slope.astype(BF16).astype(F32)

    slope_first = slope_of(first, products[:half, :half], off, products[:half, half:], norm_rows[:half])
    slope_second = slope_of(second, products[half:, half:], off_t, products[half:, :half], norm_rows[half:])
    low[:half, :half] = jnp.where(small_row == small_col, -slope_first, first).astype(BF16)
    low[:half, half:] = off.astype(BF16)
    low[half:, :half] = off_t.astype(BF16)
    low[half:, half:] = jnp.where(small_row == small_col, -slope_second, second).astype(BF16)
    slopes = jnp.concatenate([slope_first, slope_second], axis=0)
    slopes = jnp.broadcast_to(slopes, (members, 128)).reshape(groups, rows, 128)
    lines[...] = slopes
    total_first = jnp.sum(first + off, axis=1, keepdims=True)
    total_second = jnp.sum(second + off_t, axis=1, keepdims=True)
    groups_half = groups // 2
    totals[:groups_half] = jnp.broadcast_to(total_first, (half, 128)).reshape(groups_half, rows, 128)
    totals[groups_half:] = jnp.broadcast_to(total_second, (half, 128)).reshape(
        groups_half, rows, 128
    )

    def weigh(i, top):
        at = chunk_at(i)
        block = gathered[:, :, at].reshape(members, CHUNK)
        rest = jnp.dot(low[...], block, preferred_element_type=F32)
        weighted[:, :, at] = rest.reshape(groups, rows, CHUNK)
        rest = jnp.abs(rest)
        for k in range(CHUNK // 128):
            top = jnp.maximum(top, rest[:, k * 128:(k + 1) * 128])
        return top

    share_rows = rows // 2
    lane = lax.broadcasted_iota(jnp.int32, (groups, share_rows, TILE), 2)

    def give(message, base, size, d):
        other, device = group_peer(d)
        at = message * groups + d
        span = pl.ds(base, size)
        return remote(
            sent.at[other, :, span], got.at[me, :, span], r_send.at[at], r_recv.at[at], device
        )

    sizes = []
    start, base, message = 0, 0, 0
    for parts in RETURN:
        first_step, last_step = start * steps, (start + sum(parts)) * steps
        top = lax.fori_loop(first_step, last_step, weigh, jnp.zeros((members, 128), F32))
        top = jnp.max(top, axis=1, keepdims=True)
        scale = jnp.maximum(top * 1.0079, 1e-30).astype(BF16).astype(F32)
        scale = jnp.broadcast_to(scale, (members, 128)).reshape(groups, rows, 128)
        inverses[...] = RANGE / scale
        heads = jnp.where(lane < 32, scale[:, :share_rows], slopes[:, :share_rows])
        tails = jnp.where(lane < 96, scale[:, share_rows:], slopes[:, share_rows:])
        sent[:, :, base:base + TILE] = jnp.where(lane < 64, heads, tails).astype(BF16)
        first_size = TILE + 2 * parts[0] * unit

        def encode(d):
            other = group_peer(d)[0]
            inverse = inverses[other]
            place_at, step_at = base + TILE, first_step
            for eighths in parts:
                width = eighths * unit

                def code(i, _, place_at=place_at, step_at=step_at, width=width):
                    rest = weighted[other, :, chunk_at(i + step_at)]
                    coded = jnp.exp2(rest * wide(inverse)).astype(BF16)
                    early = pl.ds(pl.multiple_of(place_at + i * CHUNK, 128), CHUNK)
                    late = pl.ds(pl.multiple_of(place_at + width + i * CHUNK, 128), CHUNK)
                    sent[other, :, early] = coded[:share_rows]
                    sent[other, :, late] = coded[share_rows:]
                    return 0

                lax.fori_loop(0, eighths * steps, code, 0)
                place_at, step_at = place_at + 2 * width, step_at + eighths * steps
            give(message, base, first_size, d).start()

        each(groups, encode)
        sizes.append((base, first_size))
        base += first_size
        message += 1
        for eighths in parts[1:]:
            size = 2 * eighths * unit
            each(groups, lambda d: give(message, base, size, d).start())
            sizes.append((base, size))
            base += size
            message += 1
        start += sum(parts)

    each(chips, lambda d: obs_copy(d).wait_recv())
    obs = jnp.sqrt(jnp.sum(jnp.sum(obs_in[:chips], axis=0), axis=1, keepdims=True))
    near = jnp.broadcast_to(factor / obs, (rows, 128))
    share_factor = factor / members
    row_total = totals[me]

    def fill(piece, offset, count, along_own, value_at):
        def one(i, _):
            point = pl.ds(pl.multiple_of(piece * cols + offset + i * CHUNK, CHUNK), CHUNK)
            ours = own[:, point].astype(F32) * wide(along_own)
            out[:, point] = ours - analysis[:, point] * wide(near) + value_at(i)
            return 0

        lax.fori_loop(0, count, one, 0)

    fill(
        me, 0, cols // CHUNK, near - (row_total - lines[me]) * share_factor,
        lambda i: weighted[me, :, chunk_at(i)] * share_factor,
    )
    start = 0
    for index, eighths in enumerate(SPREAD):
        each(groups, lambda d: spread(index, start, d).wait_send())
        start += eighths
    each(chips, lambda d: obs_copy(d).wait_send())
    each(teams, lambda d: part_copy(d).wait_send())
    each(chips, lambda d: chip_copy(d).wait_send())
    each(teams, lambda d: sum_copy(d).wait_send())
    start, base, message = 0, 0, 0
    for parts in RETURN:
        tile_at = base
        base += TILE
        for nth, eighths in enumerate(parts):
            width = eighths * unit

            def take(d):
                give(message, *sizes[message], d).wait_recv()
                piece = group_source(d)

                def decode(i, scale):
                    early = pl.ds(pl.multiple_of(base + i * CHUNK, 128), CHUNK)
                    late = pl.ds(pl.multiple_of(base + width + i * CHUNK, 128), CHUNK)
                    coded = jnp.concatenate([got[piece, :, early], got[piece, :, late]], axis=0)
                    return jnp.log(coded.astype(F32)) * wide(scale)

                def add(i, _):
                    point = piece * cols + start * unit + i * CHUNK
                    point = pl.ds(pl.multiple_of(point, CHUNK), CHUNK)
                    out[:, point] += decode(i, inverses[piece])
                    return 0

                if nth:
                    lax.fori_loop(0, eighths * steps, add, 0)
                    return
                tile = got[piece, :, tile_at:tile_at + TILE].astype(F32)
                scale = jnp.concatenate([tile[:, :1], tile[:, 64:65]], axis=0)
                scale = jnp.broadcast_to(scale * (share_factor / (RANGE * LN2)), (rows, 128))
                inverses[piece] = scale
                slope = jnp.concatenate([tile[:, 32:33], tile[:, 96:97]], axis=0)
                along_own = near - (row_total - jnp.broadcast_to(slope, (rows, 128))) * share_factor
                fill(piece, start * unit, eighths * steps, along_own, lambda i: decode(i, scale))
                fill(
                    piece, (start + eighths) * unit, sum(parts[1:]) * steps, along_own,
                    lambda i: 0.0,
                )

            each(groups, take)
            if message:
                each(groups, lambda d: give(message - 1, *sizes[message - 1], d).wait_send())
            base += 2 * width
            start += eighths
            message += 1

    each(groups, lambda d: give(message - 1, *sizes[message - 1], d).wait_send())


def on_device(ensemble, analysis):
    rows, points = ensemble.shape
    groups = lax.axis_size("member")
    places = lax.axis_size("space")
    chips = places // 2
    teams = groups * 2
    members = rows * groups
    cols = points // groups
    half = members // 2
    share = members // teams
    factor = math.sqrt(points * places)
    messages = sum(len(parts) for parts in RETURN)
    dma = pltpu.SemaphoreType.DMA
    return pl.pallas_call(
        functools.partial(kernel, groups, chips, factor),
        out_shape=pltpu.VMEM((rows, points), F32),
        in_specs=[pl.BlockSpec(memory_space=pltpu.HBM)] * 2,
        out_specs=pl.BlockSpec(memory_space=pltpu.VMEM),
        scratch_shapes=[
            pltpu.VMEM((groups, rows, cols), BF16),
            pltpu.VMEM((rows, points), BF16),
            pltpu.VMEM((1, points), F32),
            pltpu.VMEM((groups, rows, cols), F32),
            pltpu.VMEM((groups, rows // 2, 2 * cols + len(RETURN) * TILE), BF16),
            pltpu.VMEM((groups, rows // 2, 2 * cols + len(RETURN) * TILE), BF16),
            pltpu.VMEM((members, members), F32),
            pltpu.VMEM((teams, share, half), F32),
            pltpu.VMEM((teams, share, half), F32),
            pltpu.VMEM((chips, share, half), F32),
            pltpu.VMEM((teams, share, half), F32),
            pltpu.VMEM((members, members), BF16),
            pltpu.VMEM((groups, rows, 128), F32),
            pltpu.VMEM((groups, rows, 128), F32),
            pltpu.VMEM((groups, rows, 128), F32),
            pltpu.VMEM((chips + 2, rows, 128), F32),
            dma((len(SPREAD) * groups,)), dma((len(SPREAD) * groups,)),
            dma((teams,)), dma((teams,)),
            dma((chips,)), dma((chips,)),
            dma((teams,)), dma((teams,)),
            dma((messages * groups,)), dma((messages * groups,)),
            dma((chips,)), dma((chips,)),
            dma((3,)),
        ],
        compiler_params=pltpu.CompilerParams(
            collective_id=0, has_side_effects=True, vmem_limit_bytes=56 * 2**20
        ),
        cost_estimate=pl.CostEstimate(
            flops=4 * members * members * cols, bytes_accessed=8 * rows * points, transcendentals=0
        ),
    )(ensemble, analysis.reshape(1, points))


def solution(mesh):
    placed = (P("member", "space"), P("space"))
    return jax.shard_map(
        on_device, mesh=mesh, in_specs=placed, out_specs=P("member", "space"), check_vma=False
    )
```
